512 devices in a mesh: cp: 64 (over y_lo, z, x), dp: 8 (over y_hi, core).
Axes of the slice: x: 4, y: 8 (y_hi: 4, y_lo: 2; y = y_hi * 2 + y_lo), z: 8, core: 2. Of those that a mesh axis runs over, the one named last changes fastest.
Arguments:
- queries: bfloat16 [8, 8192, 512], P('dp', 'cp'), may hold values from -40 to 40
- keys: bfloat16 [8, 8192, 512], P('dp', 'cp'), may hold values from -4 to 4
- values: bfloat16 [8, 8192, 512], P('dp', 'cp'), may hold values from -6 to 6
- segments: int32 [8, 8192], P('dp'), may hold values from 0 to 127, never falling along the last dimension, each value on 1 to 384 neighbouring positions
- w_out: bfloat16 [512, 1024], replicated, may hold values from -0.25 to 0.25
- cotangent: bfloat16 [8, 8192, 1024], P('dp', 'cp'), may hold values from -16 to 16
Outputs:
- query_grad: float32 [8, 8192, 512], P('dp', 'cp')
- key_grad: float32 [8, 8192, 512], P('dp', 'cp')
- value_grad: float32 [8, 8192, 512], P('dp', 'cp')
- weight_grad: float32 [512, 1024], P('cp', 'dp')
The draws below stay inside these ranges and needn't reach their ends.
Inputs may be any that keep to these rules, and one draw needn't show every extreme that they name: `segments`: in each stream the flow numbers never fall; each flow holds 1 to 384 consecutive positions and one holds exactly 384.
All inputs are finite; a program needn't handle non-finite values.
Results may differ from the reference program's by a relative error of at most 0.04.
Values may be sent and summed in bfloat16 or wider, within the bound.
A program may use at most 64 MiB of HBM per device.

```python
import math
import jax
import jax.numpy as jnp
import numpy as np
from jax import lax

D = 1024
HEADS = 4
HEAD_DIM = 128
TOK_DEV = 128
HOPS = 3
HD = 512
MOST = 384
STREAM = 8192
REPLICAS = 8
FLOWS = 128


def shared_fields(key):
    key_one = jax.random.fold_in(key, 0)
    base_keys = jnp.clip(jax.random.normal(key_one, (REPLICAS, STREAM, HD), jnp.float32), -4.0, 4.0)
    return base_keys


def draw_keys(key, part):
    base_keys = shared_fields(key)
    return base_keys.astype(jnp.bfloat16)


def draw_queries(key, part):
    key = jax.random.fold_in(key, 23)
    return jnp.clip(jax.random.normal(key, (REPLICAS, STREAM, HD), jnp.float32), -4.0, 4.0).astype(jnp.bfloat16)


def spiked(result, stream_key, source, target, shards_of, factor):
    owner, partner = [(jnp.arange(result.shape[axis_at]) // (result.shape[axis_at] // shards_of)).reshape([-1 if axis == axis_at else 1 for axis in range(result.ndim)]) for axis_at in (source, target)]
    chosen = jax.random.permutation(stream_key, shards_of)[partner]
    strong = (owner == chosen) | (owner == (partner + shards_of // 2) % shards_of)
    return jnp.where(strong, factor * result, result)


def levels(own_key, extent, cuts, low, high):
    def one(axis_at, blocks):
        draws = jax.random.uniform(jax.random.fold_in(jax.random.fold_in(own_key, 6), axis_at), (blocks,), jnp.float32, low / len(cuts), high / len(cuts))
        return jnp.repeat(jnp.exp(draws), extent[axis_at] // blocks).reshape((-1,) + (1,) * (len(extent) - axis_at - 1))

    loudness = one(*cuts[0])
    for cut in cuts[1:]:
        loudness = loudness * one(*cut)
    return loudness


def split_up(number_of, total, limit, slope):
    loads = [(1 << 20) // math.isqrt(grade ** slope) + 1 for grade in range(2, number_of + 1)]
    surplus, given = total - limit - (number_of - 1), [1] * (number_of - 1)
    while surplus > 0:
        candidates = [i for i in range(number_of - 1) if given[i] < limit]
        whole, budget = sum([loads[i] for i in candidates]), surplus
        for i in candidates:
            extra = min(limit - given[i], max(1, budget * loads[i] // whole), surplus)
            given[i] = given[i] + extra
            surplus = surplus - extra
    return np.array([limit] + given)


def uneven_parts(own_key, count, total, bound, lean):
    if count == 2:
        one = jax.random.randint(own_key, (), max(1, total - bound), min(bound, total - 1) + 1)
        return jnp.stack([one, total - one])
    lengths = jnp.asarray(split_up(count, total, bound, lean), jnp.int32)
    twos = (count - 1) // 2
    donor, taker = lengths[1:1 + 2 * twos:2], lengths[2:2 + 2 * twos:2]
    margin = jnp.minimum(donor - 1, bound - taker)
    passed = jax.random.randint(jax.random.fold_in(own_key, 1), (twos,), 0, 1 << 20) % (margin + 1)
    lengths = lengths.at[1:1 + 2 * twos:2].set(donor - passed).at[2:2 + 2 * twos:2].set(taker + passed)
    return lengths[jax.random.permutation(jax.random.fold_in(own_key, 2), count)]


def scatter_about(own_key, shape, width, most, cuts=(), held_as=jnp.bfloat16):
    gain = levels(own_key, shape, cuts, -0.22, 0.18) if cuts else 1.0
    entries = jax.random.normal(own_key, shape, jnp.float32) * width * gain
    return jnp.minimum(jnp.maximum(entries, -most), most).astype(held_as)


def gaussian_with(key, extent, scale, reach, cuts, heavy, kind=jnp.bfloat16):
    values = scale * jax.random.normal(key, extent, jnp.float32)
    if cuts:
        values = values * levels(key, extent, cuts, -0.22, 0.18)
    return jnp.clip(spiked(values, jax.random.fold_in(key, 3), *heavy), -reach, reach).astype(kind)


def setup_inputs(seed: int = 0) -> dict:
    key_of = jax.random.split(jax.random.key(seed), 7)
    return {
        "queries": draw_queries(jax.random.fold_in(key_of[6], 71), 0),
        "keys": draw_keys(jax.random.fold_in(key_of[6], 71), 0),
        "values": scatter_about(key_of[2], (REPLICAS, STREAM, HD), 1.0, 6.0, ((0, 8), (1, 64))),
        "segments": jax.vmap(lambda own: jnp.searchsorted(jnp.cumsum(uneven_parts(own, FLOWS, STREAM, MOST, 2)), jnp.arange(STREAM), side="right"))(jax.random.split(key_of[3], REPLICAS)).reshape((REPLICAS, STREAM)).astype(jnp.int32),
        "w_out": scatter_about(key_of[4], (HD, D), HD ** -0.5, 0.25),
        "cotangent": gaussian_with(key_of[5], (REPLICAS, STREAM, D), 1.0, 16.0, ((0, 8), (1, 64)), (1, 2, 64, 4.0)),
    }


NEGATIVE = -1e+30

def log_total(scores):
    highest = lax.optimization_barrier(jnp.max(scores, axis=-1, keepdims=True))
    summed = lax.optimization_barrier(jnp.sum(jnp.exp(scores - highest), axis=-1, keepdims=True))
    return highest + jnp.log(summed)

def one_stream(inputs, w_out):
    query_matrix, key_rows, value_rows, segment_row, cot_rows = inputs
    score_scale = HEAD_DIM ** (-0.5)
    causal_span = HOPS * TOK_DEV
    span_length = causal_span + TOK_DEV
    key_padded = jnp.concatenate([jnp.zeros((causal_span, HD), jnp.bfloat16), key_rows], axis=0)
    value_padded = jnp.concatenate([jnp.zeros((causal_span, HD), jnp.bfloat16), value_rows], axis=0)
    segment_padded = jnp.concatenate([-jnp.ones((causal_span,), jnp.int32), segment_row.astype(jnp.int32)], axis=0)
    d_attended_all = jnp.dot(cot_rows, w_out.T, preferred_element_type=jnp.float32).astype(jnp.bfloat16)

    def block_step(carried, block_index):
        key_acc, value_acc = carried
        offset = (block_index * TOK_DEV).astype(jnp.int32)
        query_block = lax.dynamic_slice_in_dim(query_matrix, offset, TOK_DEV, 0)
        key_block = lax.dynamic_slice_in_dim(key_padded, offset, span_length, 0)
        value_block = lax.dynamic_slice_in_dim(value_padded, offset, span_length, 0)
        d_attended = lax.dynamic_slice_in_dim(d_attended_all, offset, TOK_DEV, 0)
        query_segs = lax.dynamic_slice_in_dim(segment_padded, offset + causal_span, TOK_DEV, 0)
        key_segs = lax.dynamic_slice_in_dim(segment_padded, offset, span_length, 0)
        query_pos = offset + jnp.arange(TOK_DEV, dtype=jnp.int32)
        key_pos = offset - causal_span + jnp.arange(span_length, dtype=jnp.int32)
        visible = (query_segs[:, None] == key_segs[None, :]) & (key_pos[None, :] <= query_pos[:, None]) & (key_pos[None, :] >= 0)
        query_heads = query_block.astype(jnp.float32).reshape(TOK_DEV, HEADS, HEAD_DIM)
        key_heads = key_block.astype(jnp.float32).reshape(span_length, HEADS, HEAD_DIM)
        value_heads = value_block.astype(jnp.float32).reshape(span_length, HEADS, HEAD_DIM)
        raw_scores = jnp.einsum('qhd,khd->hqk', query_heads, key_heads)
        scores = jnp.where(visible[None], raw_scores * score_scale, NEGATIVE)
        weights = jnp.exp(scores - log_total(scores))
        rounded_probs = lax.optimization_barrier(weights.astype(jnp.bfloat16)).astype(jnp.float32)
        attention_output = jnp.einsum('hqk,khd->qhd', rounded_probs, value_heads).astype(jnp.bfloat16)
        attended_wide = lax.optimization_barrier(attention_output).astype(jnp.float32)
        grad_heads = d_attended.astype(jnp.float32).reshape(TOK_DEV, HEADS, HEAD_DIM)
        row_delta = jnp.einsum('qhd,qhd->hq', grad_heads, attended_wide)[..., None]
        d_probs = jnp.einsum('qhd,khd->hqk', grad_heads, value_heads)
        d_scores = lax.optimization_barrier((weights * (d_probs - row_delta)).astype(jnp.bfloat16)).astype(jnp.float32)
        query_grad = (jnp.einsum('hqk,khd->qhd', d_scores, key_heads) * score_scale).reshape(TOK_DEV, HD)
        key_terms = (jnp.einsum('hqk,qhd->khd', d_scores, query_heads) * score_scale).reshape(span_length, HD)
        value_terms = jnp.einsum('hqk,qhd->khd', rounded_probs, grad_heads).reshape(span_length, HD)
        key_acc = lax.dynamic_update_slice_in_dim(key_acc, lax.dynamic_slice_in_dim(key_acc, offset, span_length, 0) + key_terms, offset, 0)
        value_acc = lax.dynamic_update_slice_in_dim(value_acc, lax.dynamic_slice_in_dim(value_acc, offset, span_length, 0) + value_terms, offset, 0)
        return ((key_acc, value_acc), (query_grad, attention_output.reshape(TOK_DEV, HD)))
    zeros_acc = jnp.zeros((STREAM + causal_span, HD), jnp.float32)
    block_ids = jnp.arange(STREAM // TOK_DEV, dtype=jnp.int32)
    (key_acc, value_acc), (query_grad, attention_output) = lax.scan(block_step, (zeros_acc, zeros_acc), block_ids)
    return (query_grad.reshape(STREAM, HD), key_acc[causal_span:], value_acc[causal_span:], attention_output.reshape(STREAM, HD))

def reference(queries, keys, values, segments, w_out, cotangent):

    def per_stream(inputs):
        return one_stream(inputs, w_out)
    query_grad, key_grad, value_grad, attention_output = lax.map(per_stream, (queries, keys, values, segments, cotangent))
    weight_grad = jnp.dot(attention_output.reshape(REPLICAS * STREAM, HD).T, cotangent.reshape(REPLICAS * STREAM, D), preferred_element_type=jnp.float32) / math.sqrt(REPLICAS * STREAM)
    return (query_grad, key_grad, value_grad, weight_grad)
```

```python
import math

import jax
import jax.numpy as jnp
from jax import lax
from jax.experimental import pallas as pl
from jax.experimental.pallas import tpu as pltpu
from jax.sharding import PartitionSpec as P

HEAD_DIM = 128
ROWS = 128
MESH = pl.DeviceIdType.MESH
NEGATIVE = -1e30
F32 = jnp.float32
BF16 = jnp.bfloat16

XS = 4
PLANES = 16
PEERS = 36


def dot(left, right, left_dim, right_dim):
    return lax.dot_general(
        left, right, (((left_dim,), (right_dim,)), ((), ())), preferred_element_type=F32
    )


def kernel(
    q_hbm, k_hbm, v_hbm, seg_hbm, w_hbm, cot_hbm,
    dq_hbm, dk_hbm, dv_hbm, wg_hbm,
    kvq, seg, w_out, cot, cot_other, cots, pack_kv, pack_q, pack_do,
    pass_kv, pass_q, pass_do, own_kv, own_q, own_do, prv, outp, outn, home, nxt,
    weights_of, dk_acc, dv_acc, att,
    ya_parts, ya_got, zb_parts, zb_got, a_sum, b_sum, fin_got, results, wg_result,
    load_sem, store_sem,
    kv_send, kv_recv, q_send, q_recv, do_send, do_recv, prv_send, prv_recv,
    swap_send, swap_recv, cot_send, cot_recv, att_send, att_recv,
    home_send, home_recv, nxt_send, nxt_recv,
    ya_send, ya_recv, zb_send, zb_recv, fin_send, fin_recv, ready,
):
    cp = lax.axis_index("cp")
    dp = lax.axis_index("dp")
    x = lax.rem(cp, XS)
    plane = lax.div(cp, XS)
    z = lax.rem(plane, 8)
    y_lo = lax.div(plane, 8)
    core = lax.rem(dp, 2)
    other = dp + 1 - 2 * core
    y = lax.div(dp, 2) * 2 + y_lo
    plane_next = lax.rem(plane + 1, PLANES)
    plane_before = lax.rem(plane + PLANES - 1, PLANES)

    beside = x + 1 - 2 * lax.rem(x, 2)
    across = 3 - x
    opposite = lax.rem(x + 2, XS)
    x_high, z_high = lax.div(x, 2), lax.div(z, 4)
    side = (1 - z_high) * (1 - x_high) + z_high * x_high
    to_plane = x_high * 8 + lax.rem(x, 2) * 4
    owners = [((to_plane + group) * 4 + 2 * (1 - y_lo), dp) for group in range(4)]
    owners += [
        ((to_plane + group) * 4 + 2 * (1 - side) + 1, lax.rem(z, 4) * 2 + core)
        for group in range(4)
    ]
    head_from = 2 * y_lo + z_high
    z_from = lax.div(dp, 2) + 4 * ((1 - x_high) * y_lo + x_high * (1 - y_lo))
    odd_x = lax.rem(x, 2)
    summers = []
    for k in range(8):
        over_z = ((1 - x_high) * 8 + k) * 4 + head_from
        over_y = (k % 2 * 8 + z_from) * 4 + head_from
        summers.append(
            (over_z + odd_x * (over_y - over_z), dp + odd_x * (k // 2 * 2 + core - dp))
        )

    def along_x(step):
        return plane * XS + lax.rem(x + step, XS)

    def along_y(step):
        there = lax.rem(y + step, 8)
        return (lax.rem(there, 2) * 32 + z * 4 + x, lax.div(there, 2) * 2 + core)

    def along_z(step):
        return ((y_lo * 8 + lax.rem(z + step, 8)) * 4 + x, dp)

    def remote(source, target, send_sem, recv_sem, device):
        return pltpu.make_async_remote_copy(
            src_ref=source,
            dst_ref=target,
            send_sem=send_sem,
            recv_sem=recv_sem,
            device_id=device,
            device_id_type=MESH,
        )

    loads = [
        pltpu.make_async_copy(k_hbm, kvq.at[0], load_sem.at[0]),
        pltpu.make_async_copy(v_hbm, kvq.at[1], load_sem.at[1]),
        pltpu.make_async_copy(q_hbm, kvq.at[2], load_sem.at[2]),
        pltpu.make_async_copy(cot_hbm, cot, load_sem.at[3]),
        pltpu.make_async_copy(w_hbm, w_out, load_sem.at[4]),
        pltpu.make_async_copy(seg_hbm, seg, load_sem.at[5]),
    ]
    for load in loads:
        load.start()

    barrier = pltpu.get_barrier_semaphore()
    peers = [(along_x(step), dp) for step in range(1, XS)]
    peers += [(cp, other)] + owners + summers
    peers += [(plane_next * XS + x, dp), (plane_before * XS + x, dp)]
    peers += [along_y(step) for step in range(1, 8)]
    peers += [along_z(step) for step in range(1, 8)]
    for peer in peers:
        pl.semaphore_signal(barrier, inc=1, device_id=peer, device_id_type=MESH)

    for load in loads[:3]:
        load.wait()
    for head in range(XS):
        at = slice(head * HEAD_DIM, (head + 1) * HEAD_DIM)
        pack_kv[head, 0] = kvq[0, :, at]
        pack_kv[head, 1] = kvq[1, :, at]
        pack_q[head] = kvq[2, :, at]

    pl.semaphore_wait(barrier, PEERS)

    ring = {0: beside, 1: across, 2: opposite}

    def at_x(there):
        return (plane * XS + there, dp)

    def to_ring(pack, passing, own, send_sem, recv_sem):
        direct = [
            remote(pack.at[ring[k]], own.at[x], send_sem.at[k], recv_sem.at[k], at_x(ring[k]))
            for k in range(2)
        ]
        first = remote(pack.at[opposite], passing, send_sem.at[2], recv_sem.at[2], at_x(beside))
        second = remote(passing, own.at[beside], send_sem.at[3], recv_sem.at[3], at_x(across))
        return direct + [first, second]

    kv_copies = to_ring(pack_kv, pass_kv, own_kv, kv_send, kv_recv)
    q_copies = to_ring(pack_q, pass_q, own_q, q_send, q_recv)
    do_copies = to_ring(pack_do, pass_do, own_do, do_send, do_recv)
    for copies in (kv_copies, q_copies):
        for k in (2, 0, 1):
            copies[k].start()
    own_kv[x] = pack_kv[x]
    own_q[x] = pack_q[x]

    def prv_copy(origin):
        return remote(
            own_kv.at[origin],
            prv.at[origin - 1],
            prv_send.at[origin - 1],
            prv_recv.at[origin - 1],
            (plane_next * XS + x, dp),
        )

    def pass_on(origin):
        @pl.when(origin > 0)
        def _():
            prv_copy(origin).start()

    pass_on(x)

    loads[3].wait()
    for pair in range(4):
        at = slice(pair * 128, (pair + 1) * 128)
        even = cot[:, pair * 256 : pair * 256 + 128]
        odd = cot[:, pair * 256 + 128 : (pair + 1) * 256]
        cots[x, 0, :, at] = jnp.where(core == 0, even, odd)
        cot_other[:, at] = jnp.where(core == 0, odd, even)
    swap = remote(cot_other, cots.at[x, 1], swap_send, swap_recv, (cp, other))
    swap.start()

    for load in loads[4:]:
        load.wait()
    grads = dot(cot[...], w_out[...], 1, 1).astype(BF16)
    for head in range(XS):
        pack_do[head] = grads[:, head * HEAD_DIM : (head + 1) * HEAD_DIM]
    own_do[x] = pack_do[x]

    for copies in (kv_copies, q_copies):
        copies[2].wait_recv()
        copies[3].start()

    def cot_copy(part, kind, origin, target):
        return remote(
            cots.at[origin, part],
            cots.at[origin, part],
            cot_send.at[part, kind],
            cot_recv.at[part, kind],
            at_x(target),
        )

    cot_copies = [
        [cot_copy(part, 0, x, beside), cot_copy(part, 1, x, across)] for part in range(2)
    ]
    cot_copies[0].append(cot_copy(0, 2, beside, across))
    cot_copies[1].append(cot_copy(1, 2, across, beside))
    for k in range(2):
        cot_copies[0][k].start()
    for k in (2, 0, 1):
        do_copies[k].start()
    swap.wait_recv()
    for k in range(2):
        cot_copies[1][k].start()

    before = jnp.where(
        plane > 0,
        seg[0:1, pl.ds(pl.multiple_of(jnp.maximum(plane * 512 - 384, 0), 128), 384)],
        -1,
    )
    here = seg[0:1, pl.ds(pl.multiple_of(plane * 512, 128), 512)]
    span = jnp.concatenate([before, here], axis=1).astype(F32)
    row_at = lax.broadcasted_iota(jnp.int32, (ROWS, 4 * ROWS), 0)
    column_at = lax.broadcasted_iota(jnp.int32, (ROWS, 4 * ROWS), 1)
    causal = column_at <= row_at + 3 * ROWS

    for k, copy in zip(range(3), (kv_copies[0], kv_copies[1], kv_copies[3])):
        copy.wait_recv()
        pass_on(ring[k])
    for k in (0, 1, 3):
        q_copies[k].wait_recv()

    scale = HEAD_DIM ** (-0.5)

    def window(block, kind):
        slots = [
            prv[index, kind] if index < 3 else own_kv[index - 3, kind]
            for index in range(block, block + 4)
        ]
        return jnp.concatenate(slots, axis=0)

    def att_copy(block):
        return remote(
            att.at[0, block], att.at[1, block], att_send.at[block], att_recv.at[block], (cp, other)
        )

    for block in (3, 2, 1, 0):
        if block < 3:
            prv_copy(block + 1).wait_recv()
        query_segs = jnp.broadcast_to(
            span[:, (3 + block) * ROWS : (4 + block) * ROWS], (ROWS, ROWS)
        ).T
        query_segs = jnp.concatenate([query_segs] * 4, axis=1)
        visible = (span[:, block * ROWS : (block + 4) * ROWS] == query_segs) & causal
        raw = dot(own_q[block], window(block, 0), 1, 1) * scale
        scores = jnp.where(visible, raw, NEGATIVE)
        highest = jnp.max(scores, axis=1, keepdims=True)
        raised = jnp.exp(scores - highest)
        weights = raised * (1.0 / jnp.sum(raised, axis=1, keepdims=True))
        weights_of[block] = weights
        att[0, block] = dot(weights.astype(BF16), window(block, 1), 1, 0).astype(BF16)
        att_copy(block).start()
        if block == 3:
            do_copies[2].wait_recv()
            do_copies[3].start()

    cot_copies[0][0].wait_recv()
    cot_copies[0][2].start()
    cot_copies[1][1].wait_recv()
    cot_copies[1][2].start()

    def home_copy(there):
        return remote(
            outp.at[there],
            home.at[x],
            home_send.at[there],
            home_recv.at[x],
            (plane * XS + there, dp),
        )

    def nxt_copy(index):
        return remote(
            outn.at[index],
            nxt.at[index],
            nxt_send.at[index],
            nxt_recv.at[index],
            (plane_before * XS + x, dp),
        )

    def backward(block):
        keys = window(block, 0)
        values = window(block, 1)
        query = own_q[block]
        grad = own_do[block]
        weights = weights_of[block]
        probs = weights.astype(BF16)
        attended = att[0, block].astype(F32)
        delta = jnp.sum(grad.astype(F32) * attended, axis=1, keepdims=True)
        d_scores = (weights * (dot(grad, values, 1, 1) - delta)).astype(BF16)
        outp[block, 0] = (dot(d_scores, keys, 1, 0) * scale).astype(BF16)
        key_terms = dot(d_scores, query, 0, 0) * scale
        value_terms = dot(probs, grad, 0, 0)
        for part in range(4):
            index = block + part
            rows = slice(part * ROWS, (part + 1) * ROWS)
            if block == max(index - 3, 0):
                dk_acc[index] = key_terms[rows]
                dv_acc[index] = value_terms[rows]
            else:
                dk_acc[index] += key_terms[rows]
                dv_acc[index] += value_terms[rows]
        if block < 3:
            outn[block, 0] = dk_acc[block].astype(BF16)
            outn[block, 1] = dv_acc[block].astype(BF16)
            nxt_copy(block).start()

    def send_home(block):
        @pl.when(x != block)
        def _():
            home_copy(block).start()

    for k in (0, 1, 3):
        do_copies[k].wait_recv()
    for block in range(3):
        backward(block)

    cot_copies[0][1].wait_recv()
    cot_copies[1][0].wait_recv()
    for part in range(2):
        cot_copies[part][2].wait_recv()
    pl.semaphore_signal(ready, inc=1, device_id=(cp, other), device_id_type=MESH)
    for block in range(XS):
        att_copy(block).wait_recv()
    features = jnp.concatenate(
        [att[part, block] for part in range(2) for block in range(XS)], axis=0
    )
    columns = jnp.concatenate(
        [cots[block, part] for part in range(2) for block in range(XS)], axis=0
    )
    product = dot(features, columns, 0, 0)

    def exchange(at, device, parts, got, send_sem, recv_sem):
        return [
            remote(
                parts(lax.rem(at + step, 8)),
                got.at[step - 1],
                send_sem.at[step - 1],
                recv_sem.at[step - 1],
                device(step),
            )
            for step in range(1, 8)
        ]

    for pair in range(4):
        for half in range(2):
            for kind in range(2):
                first = half * 16 + kind * 8
                pieces = [
                    product[row : row + 8, pair * 128 : (pair + 1) * 128]
                    for row in range(first, 128, 32)
                ]
                part = jnp.concatenate(pieces, axis=0).astype(BF16)
                if kind == 0:
                    ya_parts[2 * pair + 1 - half] = part
                else:
                    zb_parts[pair + 4 * (x_high if half == 0 else 1 - x_high)] = part
    ya_copies = exchange(y, along_y, lambda at: ya_parts.at[at], ya_got, ya_send, ya_recv)
    zb_copies = exchange(z, along_z, lambda at: zb_parts.at[at], zb_got, zb_send, zb_recv)
    for pair in zip(ya_copies, zb_copies):
        for copy in pair:
            copy.start()

    backward(3)
    for there in range(XS):
        key_sum = dk_acc[there + 3]
        value_sum = dv_acc[there + 3]
        if there:
            nxt_copy(there - 1).wait_recv()
            key_sum += nxt[there - 1, 0].astype(F32)
            value_sum += nxt[there - 1, 1].astype(F32)
        outp[there, 1] = key_sum.astype(BF16)
        outp[there, 2] = value_sum.astype(BF16)
    pl.semaphore_wait(ready, 1)
    for there in range(XS):
        send_home(there)

    fin_copies = []
    for kind, (copies, parts, got, at, summed) in enumerate(
        ((ya_copies, ya_parts, ya_got, y, a_sum), (zb_copies, zb_parts, zb_got, z, b_sum))
    ):
        for copy in copies:
            copy.wait_recv()
        total = parts[at].astype(F32)
        for step in range(7):
            total += got[step].astype(F32)
        summed[...] = total
        came_along = (z, y)[kind]
        for group in range(4):
            copy = remote(
                summed.at[pl.ds(8 * group, 8)],
                fin_got.at[came_along],
                fin_send.at[4 * kind + group],
                fin_recv.at[came_along],
                owners[4 * kind + group],
            )
            copy.start()
            fin_copies.append(copy)

    for step in range(1, XS):
        there = lax.rem(x + step, XS)
        remote(
            outp.at[0],
            home.at[there],
            home_send.at[0],
            home_recv.at[there],
            (along_x(step), dp),
        ).wait_recv()
    home[x] = outp[x]

    for head in range(XS):
        at = slice(head * HEAD_DIM, (head + 1) * HEAD_DIM)
        results[0, :, at] = home[head, 0].astype(F32)
        results[1, :, at] = home[head, 1].astype(F32)
        results[2, :, at] = home[head, 2].astype(F32)
    stores = [
        pltpu.make_async_copy(results.at[index], target, store_sem.at[index])
        for index, target in enumerate((dq_hbm, dk_hbm, dv_hbm))
    ]
    for store in stores:
        store.start()

    for k in range(8):
        remote(
            a_sum.at[pl.ds(0, 8)], fin_got.at[k], fin_send.at[0], fin_recv.at[k], owners[0]
        ).wait_recv()
    total = fin_got[0]
    for k in range(1, 8):
        total += fin_got[k]
    wg_result[...] = total * (1.0 / math.sqrt(ROWS * 64 * 8))
    stores.append(pltpu.make_async_copy(wg_result, wg_hbm, store_sem.at[3]))
    stores[3].start()

    sent = kv_copies + q_copies + do_copies + [swap] + cot_copies[0] + cot_copies[1]
    for copy in sent + ya_copies + zb_copies + fin_copies:
        copy.wait_send()

    for origin in range(1, XS):
        prv_copy(origin).wait_send()
    for there in range(XS):
        att_copy(there).wait_send()

        @pl.when(x != there)
        def _(there=there):
            home_copy(there).wait_send()

    for index in range(3):
        nxt_copy(index).wait_send()
    for store in stores:
        store.wait()


def finish(*refs):
    held, held_wg, load_sem, store_sem = refs[8:]
    slots = [held.at[0], held.at[1], held.at[2], held_wg]
    loads, stores = (
        [
            pltpu.make_async_copy(source, target, sem.at[index])
            for index, (source, target) in enumerate(zip(sources, targets))
        ]
        for sources, targets, sem in (
            (refs[:4], slots, load_sem),
            (slots, refs[4:8], store_sem),
        )
    )
    for load in loads:
        load.start()
    for load, store in zip(loads, stores):
        load.wait()
        store.start()
    for store in stores:
        store.wait()


def body(queries, keys, values, segments, w_out, cotangent):
    results = [
        jax.ShapeDtypeStruct((ROWS, 512), F32),
        jax.ShapeDtypeStruct((ROWS, 512), F32),
        jax.ShapeDtypeStruct((ROWS, 512), F32),
        jax.ShapeDtypeStruct((8, 128), F32),
    ]
    dma = pltpu.SemaphoreType.DMA
    tile = (ROWS, HEAD_DIM)
    hbm = pl.BlockSpec(memory_space=pltpu.HBM)
    outs = pl.pallas_call(
        kernel,
        out_shape=results,
        in_specs=[hbm] * 6,
        out_specs=[hbm] * 4,
        scratch_shapes=[
            pltpu.VMEM((3, ROWS, 512), BF16),
            pltpu.VMEM((1, 8192), jnp.int32),
            pltpu.VMEM((512, 1024), BF16),
            pltpu.VMEM((ROWS, 1024), BF16),
            pltpu.VMEM((ROWS, 512), BF16),
            pltpu.VMEM((XS, 2, ROWS, 512), BF16),
            pltpu.VMEM((XS, 2) + tile, BF16),
            pltpu.VMEM((XS,) + tile, BF16),
            pltpu.VMEM((XS,) + tile, BF16),
            pltpu.VMEM((2,) + tile, BF16),
            pltpu.VMEM(tile, BF16),
            pltpu.VMEM(tile, BF16),
            pltpu.VMEM((XS, 2) + tile, BF16),
            pltpu.VMEM((XS,) + tile, BF16),
            pltpu.VMEM((XS,) + tile, BF16),
            pltpu.VMEM((3, 2) + tile, BF16),
            pltpu.VMEM((XS, 3) + tile, BF16),
            pltpu.VMEM((3, 2) + tile, BF16),
            pltpu.VMEM((XS, 3) + tile, BF16),
            pltpu.VMEM((3, 2) + tile, BF16),
            pltpu.VMEM((XS, ROWS, 4 * ROWS), F32),
            pltpu.VMEM((7,) + tile, F32),
            pltpu.VMEM((7,) + tile, F32),
            pltpu.VMEM((2, XS) + tile, BF16),
            pltpu.VMEM((8, 32, 128), BF16),
            pltpu.VMEM((7, 32, 128), BF16),
            pltpu.VMEM((8, 32, 128), BF16),
            pltpu.VMEM((7, 32, 128), BF16),
            pltpu.VMEM((32, 128), F32),
            pltpu.VMEM((32, 128), F32),
            pltpu.VMEM((8, 8, 128), F32),
            pltpu.VMEM((3, ROWS, 512), F32),
            pltpu.VMEM((8, 128), F32),
            dma((6,)), dma((4,)),
            dma((4,)), dma((4,)),
            dma((4,)), dma((4,)),
            dma((4,)), dma((4,)),
            dma((3,)), dma((3,)),
            dma, dma,
            dma((2, 3)), dma((2, 3)),
            dma((4,)), dma((4,)),
            dma((4,)), dma((4,)),
            dma((3,)), dma((3,)),
            dma((7,)), dma((7,)),
            dma((7,)), dma((7,)),
            dma((8,)), dma((8,)),
            pltpu.SemaphoreType.REGULAR,
        ],
        compiler_params=pltpu.CompilerParams(
            collective_id=0, has_side_effects=True, vmem_limit_bytes=60 * 1024 * 1024
        ),
        cost_estimate=pl.CostEstimate(
            flops=600_000_000, bytes_accessed=4_000_000, transcendentals=262_144
        ),
    )(queries[0], keys[0], values[0], segments, w_out, cotangent[0])
    query_grad, key_grad, value_grad, weight_grad = pl.pallas_call(
        finish,
        out_shape=results,
        in_specs=[hbm] * 4,
        out_specs=[hbm] * 4,
        scratch_shapes=[
            pltpu.VMEM((3, ROWS, 512), F32),
            pltpu.VMEM((8, 128), F32),
            dma((4,)),
            dma((4,)),
        ],
        compiler_params=pltpu.CompilerParams(vmem_limit_bytes=60 * 1024 * 1024),
        cost_estimate=pl.CostEstimate(flops=0, bytes_accessed=1_600_000, transcendentals=0),
    )(*outs)
    return (query_grad[None], key_grad[None], value_grad[None], weight_grad)


def solution(mesh):
    in_specs = (
        P("dp", "cp", None),
        P("dp", "cp", None),
        P("dp", "cp", None),
        P("dp", None),
        P(),
        P("dp", "cp", None),
    )
    out_specs = (P("dp", "cp", None), P("dp", "cp", None), P("dp", "cp", None), P("cp", "dp"))
    return jax.shard_map(body, mesh=mesh, in_specs=in_specs, out_specs=out_specs, check_vma=False)
```

```python
import math

import jax
import jax.numpy as jnp
from jax import lax
from jax.experimental import pallas as pl
from jax.experimental.pallas import tpu as pltpu
from jax.sharding import PartitionSpec as P

HEAD_DIM = 128
ROWS = 128
MESH = pl.DeviceIdType.MESH
NEGATIVE = -1e30
F32 = jnp.float32
BF16 = jnp.bfloat16

XS = 4
PLANES = 16
PEERS = 36


def dot(left, right, left_dim, right_dim):
    return lax.dot_general(
        left, right, (((left_dim,), (right_dim,)), ((), ())), preferred_element_type=F32
    )


def kernel(
    q_hbm, k_hbm, v_hbm, seg_hbm, w_hbm, cot_hbm,
    dq_out, dk_out, dv_out, wg_out,
    kvq, seg, w_out, cot, cot_other, cots, pack_kv, pack_q, pack_do,
    pass_kv, pass_q, pass_do, own_kv, own_q, own_do, prv, out_q, out_kv, outn, home_q, home_kv, nxt,
    weights_of, dk_acc, dv_acc, att,
    ya_parts, ya_got, zb_parts, zb_got, a_sum, b_sum, fin_got,
    load_sem,
    kv_send, kv_recv, q_send, q_recv, do_send, do_recv, prv_send, prv_recv,
    swap_send, swap_recv, cot_send, cot_recv, att_send, att_recv,
    dq_send, dq_recv, home_send, home_recv, nxt_send, nxt_recv,
    ya_send, ya_recv, zb_send, zb_recv, fin_send, fin_recv, ready,
):
    cp = lax.axis_index("cp")
    dp = lax.axis_index("dp")
    x = lax.rem(cp, XS)
    plane = lax.div(cp, XS)
    z = lax.rem(plane, 8)
    y_lo = lax.div(plane, 8)
    core = lax.rem(dp, 2)
    other = dp + 1 - 2 * core
    y = lax.div(dp, 2) * 2 + y_lo
    plane_next = lax.rem(plane + 1, PLANES)
    plane_before = lax.rem(plane + PLANES - 1, PLANES)

    beside = x + 1 - 2 * lax.rem(x, 2)
    across = 3 - x
    opposite = lax.rem(x + 2, XS)
    x_high, z_high = lax.div(x, 2), lax.div(z, 4)
    side = (1 - z_high) * (1 - x_high) + z_high * x_high
    to_plane = x_high * 8 + lax.rem(x, 2) * 4
    owners = [((to_plane + group) * 4 + 2 * (1 - y_lo), dp) for group in range(4)]
    owners += [
        ((to_plane + group) * 4 + 2 * (1 - side) + 1, lax.rem(z, 4) * 2 + core)
        for group in range(4)
    ]
    head_from = 2 * y_lo + z_high
    z_from = lax.div(dp, 2) + 4 * ((1 - x_high) * y_lo + x_high * (1 - y_lo))
    odd_x = lax.rem(x, 2)
    summers = []
    for k in range(8):
        over_z = ((1 - x_high) * 8 + k) * 4 + head_from
        over_y = (k % 2 * 8 + z_from) * 4 + head_from
        summers.append(
            (over_z + odd_x * (over_y - over_z), dp + odd_x * (k // 2 * 2 + core - dp))
        )

    def along_x(step):
        return plane * XS + lax.rem(x + step, XS)

    def along_y(step):
        there = lax.rem(y + step, 8)
        return (lax.rem(there, 2) * 32 + z * 4 + x, lax.div(there, 2) * 2 + core)

    def along_z(step):
        return ((y_lo * 8 + lax.rem(z + step, 8)) * 4 + x, dp)

    def remote(source, target, send_sem, recv_sem, device):
        return pltpu.make_async_remote_copy(
            src_ref=source,
            dst_ref=target,
            send_sem=send_sem,
            recv_sem=recv_sem,
            device_id=device,
            device_id_type=MESH,
        )

    loads = [
        pltpu.make_async_copy(k_hbm, kvq.at[0], load_sem.at[0]),
        pltpu.make_async_copy(v_hbm, kvq.at[1], load_sem.at[1]),
        pltpu.make_async_copy(q_hbm, kvq.at[2], load_sem.at[2]),
        pltpu.make_async_copy(cot_hbm, cot, load_sem.at[3]),
        pltpu.make_async_copy(w_hbm, w_out, load_sem.at[4]),
        pltpu.make_async_copy(seg_hbm, seg, load_sem.at[5]),
    ]
    for load in loads:
        load.start()

    barrier = pltpu.get_barrier_semaphore()
    peers = [(along_x(step), dp) for step in range(1, XS)]
    peers += [(cp, other)] + owners + summers
    peers += [(plane_next * XS + x, dp), (plane_before * XS + x, dp)]
    peers += [along_y(step) for step in range(1, 8)]
    peers += [along_z(step) for step in range(1, 8)]
    for peer in peers:
        pl.semaphore_signal(barrier, inc=1, device_id=peer, device_id_type=MESH)

    for load in loads[:3]:
        load.wait()
    for head in range(XS):
        at = slice(head * HEAD_DIM, (head + 1) * HEAD_DIM)
        pack_kv[head, 0] = kvq[0, :, at]
        pack_kv[head, 1] = kvq[1, :, at]
        pack_q[head] = kvq[2, :, at]

    pl.semaphore_wait(barrier, PEERS)

    ring = {0: beside, 1: across, 2: opposite}

    def at_x(there):
        return (plane * XS + there, dp)

    def to_ring(pack, passing, own, send_sem, recv_sem):
        direct = [
            remote(pack.at[ring[k]], own.at[x], send_sem.at[k], recv_sem.at[k], at_x(ring[k]))
            for k in range(2)
        ]
        first = remote(pack.at[opposite], passing, send_sem.at[2], recv_sem.at[2], at_x(beside))
        second = remote(passing, own.at[beside], send_sem.at[3], recv_sem.at[3], at_x(across))
        return direct + [first, second]

    kv_copies = to_ring(pack_kv, pass_kv, own_kv, kv_send, kv_recv)
    q_copies = to_ring(pack_q, pass_q, own_q, q_send, q_recv)
    do_copies = to_ring(pack_do, pass_do, own_do, do_send, do_recv)
    for copies in (kv_copies, q_copies):
        for k in (2, 0, 1):
            copies[k].start()
    own_kv[x] = pack_kv[x]
    own_q[x] = pack_q[x]

    def prv_copy(origin):
        return remote(
            own_kv.at[origin],
            prv.at[origin - 1],
            prv_send.at[origin - 1],
            prv_recv.at[origin - 1],
            (plane_next * XS + x, dp),
        )

    def pass_on(origin):
        @pl.when(origin > 0)
        def _():
            prv_copy(origin).start()

    pass_on(x)

    loads[3].wait()
    for pair in range(4):
        at = slice(pair * 128, (pair + 1) * 128)
        even = cot[:, pair * 256 : pair * 256 + 128]
        odd = cot[:, pair * 256 + 128 : (pair + 1) * 256]
        cots[x, 0, :, at] = jnp.where(core == 0, even, odd)
        cot_other[:, at] = jnp.where(core == 0, odd, even)
    swap = remote(cot_other, cots.at[x, 1], swap_send, swap_recv, (cp, other))
    swap.start()

    for load in loads[4:]:
        load.wait()
    grads = dot(cot[...], w_out[...], 1, 1).astype(BF16)
    for head in range(XS):
        pack_do[head] = grads[:, head * HEAD_DIM : (head + 1) * HEAD_DIM]
    own_do[x] = pack_do[x]

    for copies in (kv_copies, q_copies):
        copies[2].wait_recv()
        copies[3].start()

    def cot_copy(part, kind, origin, target):
        return remote(
            cots.at[origin, part],
            cots.at[origin, part],
            cot_send.at[part, kind],
            cot_recv.at[part, kind],
            at_x(target),
        )

    cot_copies = [
        [cot_copy(part, 0, x, beside), cot_copy(part, 1, x, across)] for part in range(2)
    ]
    cot_copies[0].append(cot_copy(0, 2, beside, across))
    cot_copies[1].append(cot_copy(1, 2, across, beside))
    for k in range(2):
        cot_copies[0][k].start()
    for k in (2, 0, 1):
        do_copies[k].start()
    swap.wait_recv()
    for k in range(2):
        cot_copies[1][k].start()

    before = jnp.where(
        plane > 0,
        seg[0:1, pl.ds(pl.multiple_of(jnp.maximum(plane * 512 - 384, 0), 128), 384)],
        -1,
    )
    here = seg[0:1, pl.ds(pl.multiple_of(plane * 512, 128), 512)]
    span = jnp.concatenate([before, here], axis=1).astype(F32)
    row_at = lax.broadcasted_iota(jnp.int32, (ROWS, 4 * ROWS), 0)
    column_at = lax.broadcasted_iota(jnp.int32, (ROWS, 4 * ROWS), 1)
    causal = column_at <= row_at + 3 * ROWS

    for k, copy in zip(range(3), (kv_copies[0], kv_copies[1], kv_copies[3])):
        copy.wait_recv()
        pass_on(ring[k])
    for k in (0, 1, 3):
        q_copies[k].wait_recv()

    scale = HEAD_DIM ** (-0.5)

    def window(block, kind):
        slots = [
            prv[index, kind] if index < 3 else own_kv[index - 3, kind]
            for index in range(block, block + 4)
        ]
        return jnp.concatenate(slots, axis=0)

    att_copy = remote(att.at[0], att.at[1], att_send, att_recv, (cp, other))

    def forward(block):
        query_segs = jnp.broadcast_to(
            span[:, (3 + block) * ROWS : (4 + block) * ROWS], (ROWS, ROWS)
        ).T
        query_segs = jnp.concatenate([query_segs] * 4, axis=1)
        visible = (span[:, block * ROWS : (block + 4) * ROWS] == query_segs) & causal
        raw = dot(own_q[block], window(block, 0), 1, 1) * scale
        scores = jnp.where(visible, raw, NEGATIVE)
        highest = jnp.max(scores, axis=1, keepdims=True)
        raised = jnp.exp(scores - highest)
        weights = raised * (1.0 / jnp.sum(raised, axis=1, keepdims=True))
        weights_of[block] = weights
        att[0, block] = dot(weights.astype(BF16), window(block, 1), 1, 0).astype(BF16)

    forward(3)
    do_copies[2].wait_recv()
    do_copies[3].start()
    for origin in range(1, XS):
        prv_copy(origin).wait_recv()
    for block in (2, 1, 0):
        forward(block)
    att_copy.start()

    cot_copies[0][0].wait_recv()
    cot_copies[0][2].start()
    cot_copies[1][1].wait_recv()
    cot_copies[1][2].start()

    def dq_copy(there):
        return remote(
            out_q.at[there],
            home_q.at[x],
            dq_send.at[there],
            dq_recv.at[x],
            (plane * XS + there, dp),
        )

    def home_copy(there):
        return remote(
            out_kv.at[there],
            home_kv.at[x],
            home_send.at[there],
            home_recv.at[x],
            (plane * XS + there, dp),
        )

    def nxt_copy(index):
        return remote(
            outn.at[index],
            nxt.at[index],
            nxt_send.at[index],
            nxt_recv.at[index],
            (plane_before * XS + x, dp),
        )

    def backward(block):
        keys = window(block, 0)
        values = window(block, 1)
        query = own_q[block]
        grad = own_do[block]
        weights = weights_of[block]
        probs = weights.astype(BF16)
        attended = att[0, block].astype(F32)
        delta = jnp.sum(grad.astype(F32) * attended, axis=1, keepdims=True)
        d_scores = (weights * (dot(grad, values, 1, 1) - delta)).astype(BF16)
        out_q[block] = (dot(d_scores, keys, 1, 0) * scale).astype(BF16)
        key_terms = dot(d_scores, query, 0, 0) * scale
        value_terms = dot(probs, grad, 0, 0)
        for part in range(4):
            index = block + part
            rows = slice(part * ROWS, (part + 1) * ROWS)
            if block == max(index - 3, 0):
                dk_acc[index] = key_terms[rows]
                dv_acc[index] = value_terms[rows]
            else:
                dk_acc[index] += key_terms[rows]
                dv_acc[index] += value_terms[rows]
        if block < 3:
            outn[block, 0] = dk_acc[block].astype(BF16)
            outn[block, 1] = dv_acc[block].astype(BF16)

    def send_home(copy, block):
        @pl.when(x != block)
        def _():
            copy(block).start()

    for k in (0, 1, 3):
        do_copies[k].wait_recv()
    backward(0)
    nxt_copy(0).start()

    cot_copies[0][1].wait_recv()
    cot_copies[1][0].wait_recv()
    for part in range(2):
        cot_copies[part][2].wait_recv()
    pl.semaphore_signal(ready, inc=1, device_id=(cp, other), device_id_type=MESH)
    att_copy.wait_recv()
    features = jnp.concatenate(
        [att[part, block] for part in range(2) for block in range(XS)], axis=0
    )
    columns = jnp.concatenate(
        [cots[block, part] for part in range(2) for block in range(XS)], axis=0
    )
    product = dot(features, columns, 0, 0)

    def exchange(at, device, parts, got, send_sem, recv_sem):
        return [
            remote(
                parts(lax.rem(at + step, 8)),
                got.at[step - 1],
                send_sem.at[step - 1],
                recv_sem.at[step - 1],
                device(step),
            )
            for step in range(1, 8)
        ]

    for pair in range(4):
        for half in range(2):
            for kind in range(2):
                first = half * 16 + kind * 8
                pieces = [
                    product[row : row + 8, pair * 128 : (pair + 1) * 128]
                    for row in range(first, 128, 32)
                ]
                part = jnp.concatenate(pieces, axis=0).astype(BF16)
                if kind == 0:
                    ya_parts[2 * pair + 1 - half] = part
                else:
                    zb_parts[pair + 4 * (x_high if half == 0 else 1 - x_high)] = part
    ya_copies = exchange(y, along_y, lambda at: ya_parts.at[at], ya_got, ya_send, ya_recv)
    zb_copies = exchange(z, along_z, lambda at: zb_parts.at[at], zb_got, zb_send, zb_recv)
    for pair in zip(ya_copies, zb_copies):
        for copy in pair:
            copy.start()

    backward(1)
    backward(2)
    for block in (1, 2):
        nxt_copy(block).start()
    pl.semaphore_wait(ready, 1)
    for block in range(3):
        send_home(dq_copy, block)

    fin_copies = []
    for kind, (copies, parts, got, at, summed) in enumerate(
        ((ya_copies, ya_parts, ya_got, y, a_sum), (zb_copies, zb_parts, zb_got, z, b_sum))
    ):
        for copy in copies:
            copy.wait_recv()
        total = parts[at].astype(F32)
        for step in range(7):
            total += got[step].astype(F32)
        summed[...] = total
        came_along = (z, y)[kind]
        for group in range(4):
            copy = remote(
                summed.at[pl.ds(8 * group, 8)],
                fin_got.at[came_along],
                fin_send.at[4 * kind + group],
                fin_recv.at[came_along],
                owners[4 * kind + group],
            )
            copy.start()
            fin_copies.append(copy)

    backward(3)
    send_home(dq_copy, 3)
    for there in range(XS):
        key_sum = dk_acc[there + 3]
        value_sum = dv_acc[there + 3]
        if there:
            nxt_copy(there - 1).wait_recv()
            key_sum += nxt[there - 1, 0].astype(F32)
            value_sum += nxt[there - 1, 1].astype(F32)
        out_kv[there, 0] = key_sum.astype(BF16)
        out_kv[there, 1] = value_sum.astype(BF16)
    for there in range(XS):
        send_home(home_copy, there)

    for step in range(1, XS):
        there = lax.rem(x + step, XS)
        for source, target, send_sem, recv_sem in (
            (out_q, home_q, dq_send, dq_recv),
            (out_kv, home_kv, home_send, home_recv),
        ):
            remote(
                source.at[0],
                target.at[there],
                send_sem.at[0],
                recv_sem.at[there],
                (along_x(step), dp),
            ).wait_recv()
    home_q[x] = out_q[x]
    home_kv[x] = out_kv[x]

    for head in range(XS):
        at = slice(head * HEAD_DIM, (head + 1) * HEAD_DIM)
        dq_out[:, at] = home_q[head].astype(F32)
        dk_out[:, at] = home_kv[head, 0].astype(F32)
        dv_out[:, at] = home_kv[head, 1].astype(F32)
    for k in range(8):
        remote(
            a_sum.at[pl.ds(0, 8)], fin_got.at[k], fin_send.at[0], fin_recv.at[k], owners[0]
        ).wait_recv()
    total = fin_got[0]
    for k in range(1, 8):
        total += fin_got[k]
    wg_out[...] = total * (1.0 / math.sqrt(ROWS * 64 * 8))

    sent = kv_copies + q_copies + do_copies + [swap, att_copy] + cot_copies[0] + cot_copies[1]
    for copy in sent + ya_copies + zb_copies + fin_copies:
        copy.wait_send()

    for origin in range(1, XS):
        prv_copy(origin).wait_send()
    for there in range(XS):

        @pl.when(x != there)
        def _(there=there):
            dq_copy(there).wait_send()
            home_copy(there).wait_send()

    for index in range(3):
        nxt_copy(index).wait_send()


def finish(*refs):
    copies = [
        pltpu.make_async_copy(refs[index], refs[4 + index], refs[8].at[index])
        for index in range(4)
    ]
    for copy in copies:
        copy.start()
    for copy in copies:
        copy.wait()


def body(queries, keys, values, segments, w_out, cotangent):
    results = [
        jax.ShapeDtypeStruct((ROWS, 512), F32),
        jax.ShapeDtypeStruct((ROWS, 512), F32),
        jax.ShapeDtypeStruct((ROWS, 512), F32),
        jax.ShapeDtypeStruct((8, 128), F32),
    ]
    dma = pltpu.SemaphoreType.DMA
    tile = (ROWS, HEAD_DIM)
    hbm = pl.BlockSpec(memory_space=pltpu.HBM)
    vmem = pl.BlockSpec(memory_space=pltpu.VMEM)
    operands = [queries[0], keys[0], values[0], segments, w_out, cotangent[0]]
    operands = [pltpu.with_memory_space_constraint(operand, pltpu.HBM) for operand in operands]
    outs = pl.pallas_call(
        kernel,
        out_shape=[pltpu.VMEM(result.shape, result.dtype) for result in results],
        in_specs=[hbm] * 6,
        out_specs=[vmem] * 4,
        scratch_shapes=[
            pltpu.VMEM((3, ROWS, 512), BF16),
            pltpu.VMEM((1, 8192), jnp.int32),
            pltpu.VMEM((512, 1024), BF16),
            pltpu.VMEM((ROWS, 1024), BF16),
            pltpu.VMEM((ROWS, 512), BF16),
            pltpu.VMEM((XS, 2, ROWS, 512), BF16),
            pltpu.VMEM((XS, 2) + tile, BF16),
            pltpu.VMEM((XS,) + tile, BF16),
            pltpu.VMEM((XS,) + tile, BF16),
            pltpu.VMEM((2,) + tile, BF16),
            pltpu.VMEM(tile, BF16),
            pltpu.VMEM(tile, BF16),
            pltpu.VMEM((XS, 2) + tile, BF16),
            pltpu.VMEM((XS,) + tile, BF16),
            pltpu.VMEM((XS,) + tile, BF16),
            pltpu.VMEM((3, 2) + tile, BF16),
            pltpu.VMEM((XS,) + tile, BF16),
            pltpu.VMEM((XS, 2) + tile, BF16),
            pltpu.VMEM((3, 2) + tile, BF16),
            pltpu.VMEM((XS,) + tile, BF16),
            pltpu.VMEM((XS, 2) + tile, BF16),
            pltpu.VMEM((3, 2) + tile, BF16),
            pltpu.VMEM((XS, ROWS, 4 * ROWS), F32),
            pltpu.VMEM((7,) + tile, F32),
            pltpu.VMEM((7,) + tile, F32),
            pltpu.VMEM((2, XS) + tile, BF16),
            pltpu.VMEM((8, 32, 128), BF16),
            pltpu.VMEM((7, 32, 128), BF16),
            pltpu.VMEM((8, 32, 128), BF16),
            pltpu.VMEM((7, 32, 128), BF16),
            pltpu.VMEM((32, 128), F32),
            pltpu.VMEM((32, 128), F32),
            pltpu.VMEM((8, 8, 128), F32),
            dma((6,)),
            dma((4,)), dma((4,)),
            dma((4,)), dma((4,)),
            dma((4,)), dma((4,)),
            dma((3,)), dma((3,)),
            dma, dma,
            dma((2, 3)), dma((2, 3)),
            dma, dma,
            dma((4,)), dma((4,)),
            dma((4,)), dma((4,)),
            dma((3,)), dma((3,)),
            dma((7,)), dma((7,)),
            dma((7,)), dma((7,)),
            dma((8,)), dma((8,)),
            pltpu.SemaphoreType.REGULAR,
        ],
        compiler_params=pltpu.CompilerParams(
            collective_id=0, has_side_effects=True, vmem_limit_bytes=32 * 1024 * 1024
        ),
        cost_estimate=pl.CostEstimate(
            flops=600_000_000, bytes_accessed=4_000_000, transcendentals=262_144
        ),
    )(*operands)
    query_grad, key_grad, value_grad, weight_grad = pl.pallas_call(
        finish,
        out_shape=results,
        in_specs=[vmem] * 4,
        out_specs=[hbm] * 4,
        scratch_shapes=[dma((4,))],
        compiler_params=pltpu.CompilerParams(vmem_limit_bytes=4 * 1024 * 1024),
        cost_estimate=pl.CostEstimate(flops=0, bytes_accessed=1_600_000, transcendentals=0),
    )(*outs)
    return (query_grad[None], key_grad[None], value_grad[None], weight_grad)


def solution(mesh):
    in_specs = (
        P("dp", "cp", None),
        P("dp", "cp", None),
        P("dp", "cp", None),
        P("dp", None),
        P(),
        P("dp", "cp", None),
    )
    out_specs = (P("dp", "cp", None), P("dp", "cp", None), P("dp", "cp", None), P("cp", "dp"))
    return jax.shard_map(body, mesh=mesh, in_specs=in_specs, out_specs=out_specs, check_vma=False)
```

```python
import math

import jax
import jax.numpy as jnp
from jax import lax
from jax.experimental import pallas as pl
from jax.experimental.pallas import tpu as pltpu
from jax.sharding import PartitionSpec as P

HEAD_DIM = 128
ROWS = 128
MESH = pl.DeviceIdType.MESH
NEGATIVE = -1e30
F32 = jnp.float32
BF16 = jnp.bfloat16

XS = 4
PLANES = 16
PEERS = 36


def dot(left, right, left_dim, right_dim):
    return lax.dot_general(
        left, right, (((left_dim,), (right_dim,)), ((), ())), preferred_element_type=F32
    )


def kernel(
    q_hbm, k_hbm, v_hbm, seg_hbm, w_hbm, cot_hbm,
    dq_out, dk_out, dv_out, wg_out,
    kvq, seg, w_out, cot, cot_other, cots, pack_kv, pack_q, pack_do,
    pass_kv, pass_q, pass_do, own_kv, own_q, own_do, prv, out_q, out_kv, outn, home_q, home_kv, nxt,
    weights_of, dk_acc, dv_acc, att,
    ya_parts, ya_got, zb_parts, zb_got, a_sum, b_sum, fin_got,
    load_sem,
    kv_send, kv_recv, q_send, q_recv, do_send, do_recv, prv_send, prv_recv,
    swap_send, swap_recv, cot_send, cot_recv, att_send, att_recv,
    dq_send, dq_recv, home_send, home_recv, nxt_send, nxt_recv,
    ya_send, ya_recv, zb_send, zb_recv, fin_send, fin_recv, ready,
):
    cp = lax.axis_index("cp")
    dp = lax.axis_index("dp")
    x = lax.rem(cp, XS)
    plane = lax.div(cp, XS)
    z = lax.rem(plane, 8)
    y_lo = lax.div(plane, 8)
    core = lax.rem(dp, 2)
    other = dp + 1 - 2 * core
    y = lax.div(dp, 2) * 2 + y_lo
    plane_next = lax.rem(plane + 1, PLANES)
    plane_before = lax.rem(plane + PLANES - 1, PLANES)

    beside = x + 1 - 2 * lax.rem(x, 2)
    across = 3 - x
    opposite = lax.rem(x + 2, XS)
    x_high, z_high = lax.div(x, 2), lax.div(z, 4)
    side = (1 - z_high) * (1 - x_high) + z_high * x_high
    to_plane = x_high * 8 + lax.rem(x, 2) * 4
    owners = [((to_plane + group) * 4 + 2 * (1 - y_lo), dp) for group in range(4)]
    owners += [
        ((to_plane + group) * 4 + 2 * (1 - side) + 1, lax.rem(z, 4) * 2 + core)
        for group in range(4)
    ]
    head_from = 2 * y_lo + z_high
    z_from = lax.div(dp, 2) + 4 * ((1 - x_high) * y_lo + x_high * (1 - y_lo))
    odd_x = lax.rem(x, 2)
    summers = []
    for k in range(8):
        over_z = ((1 - x_high) * 8 + k) * 4 + head_from
        over_y = (k % 2 * 8 + z_from) * 4 + head_from
        summers.append(
            (over_z + odd_x * (over_y - over_z), dp + odd_x * (k // 2 * 2 + core - dp))
        )

    def along_x(step):
        return plane * XS + lax.rem(x + step, XS)

    def along_y(step):
        there = lax.rem(y + step, 8)
        return (lax.rem(there, 2) * 32 + z * 4 + x, lax.div(there, 2) * 2 + core)

    def along_z(step):
        return ((y_lo * 8 + lax.rem(z + step, 8)) * 4 + x, dp)

    def remote(source, target, send_sem, recv_sem, device):
        return pltpu.make_async_remote_copy(
            src_ref=source,
            dst_ref=target,
            send_sem=send_sem,
            recv_sem=recv_sem,
            device_id=device,
            device_id_type=MESH,
        )

    loads = [
        pltpu.make_async_copy(k_hbm, kvq.at[0], load_sem.at[0]),
        pltpu.make_async_copy(v_hbm, kvq.at[1], load_sem.at[1]),
        pltpu.make_async_copy(q_hbm, kvq.at[2], load_sem.at[2]),
        pltpu.make_async_copy(cot_hbm, cot, load_sem.at[3]),
        pltpu.make_async_copy(w_hbm, w_out, load_sem.at[4]),
        pltpu.make_async_copy(seg_hbm, seg, load_sem.at[5]),
    ]
    for load in loads:
        load.start()

    barrier = pltpu.get_barrier_semaphore()
    peers = [(along_x(step), dp) for step in range(1, XS)]
    peers += [(cp, other)] + owners + summers
    peers += [(plane_next * XS + x, dp), (plane_before * XS + x, dp)]
    peers += [along_y(step) for step in range(1, 8)]
    peers += [along_z(step) for step in range(1, 8)]
    for peer in peers:
        pl.semaphore_signal(barrier, inc=1, device_id=peer, device_id_type=MESH)

    for load in loads[:3]:
        load.wait()
    for head in range(XS):
        at = slice(head * HEAD_DIM, (head + 1) * HEAD_DIM)
        pack_kv[head, 0] = kvq[0, :, at]
        pack_kv[head, 1] = kvq[1, :, at]
        pack_q[head] = kvq[2, :, at]

    pl.semaphore_wait(barrier, PEERS)

    ring = {0: beside, 1: across, 2: opposite}

    def at_x(there):
        return (plane * XS + there, dp)

    def to_ring(pack, passing, own, send_sem, recv_sem):
        direct = [
            remote(pack.at[ring[k]], own.at[x], send_sem.at[k], recv_sem.at[k], at_x(ring[k]))
            for k in range(2)
        ]
        first = remote(pack.at[opposite], passing, send_sem.at[2], recv_sem.at[2], at_x(beside))
        second = remote(passing, own.at[beside], send_sem.at[3], recv_sem.at[3], at_x(across))
        return direct + [first, second]

    kv_copies = to_ring(pack_kv, pass_kv, own_kv, kv_send, kv_recv)
    q_copies = to_ring(pack_q, pass_q, own_q, q_send, q_recv)
    do_copies = to_ring(pack_do, pass_do, own_do, do_send, do_recv)
    for copies in (kv_copies, q_copies):
        for k in (2, 0, 1):
            copies[k].start()
    own_kv[x] = pack_kv[x]
    own_q[x] = pack_q[x]

    def prv_copy(origin):
        return remote(
            own_kv.at[origin],
            prv.at[origin - 1],
            prv_send.at[origin - 1],
            prv_recv.at[origin - 1],
            (plane_next * XS + x, dp),
        )

    def pass_on(origin):
        @pl.when(origin > 0)
        def _():
            prv_copy(origin).start()

    pass_on(x)

    loads[3].wait()
    for pair in range(4):
        at = slice(pair * 128, (pair + 1) * 128)
        even = cot[:, pair * 256 : pair * 256 + 128]
        odd = cot[:, pair * 256 + 128 : (pair + 1) * 256]
        cots[x, 0, :, at] = jnp.where(core == 0, even, odd)
        cot_other[:, at] = jnp.where(core == 0, odd, even)
    swap = remote(cot_other, cots.at[x, 1], swap_send, swap_recv, (cp, other))
    swap.start()

    for load in loads[4:]:
        load.wait()
    grads = dot(cot[...], w_out[...], 1, 1).astype(BF16)
    for head in range(XS):
        pack_do[head] = grads[:, head * HEAD_DIM : (head + 1) * HEAD_DIM]
    own_do[x] = pack_do[x]

    for copies in (kv_copies, q_copies):
        copies[2].wait_recv()
        copies[3].start()

    def cot_copy(part, kind, origin, target):
        return remote(
            cots.at[origin, part],
            cots.at[origin, part],
            cot_send.at[part, kind],
            cot_recv.at[part, kind],
            at_x(target),
        )

    cot_copies = [
        [cot_copy(part, 0, x, beside), cot_copy(part, 1, x, across)] for part in range(2)
    ]
    cot_copies[0].append(cot_copy(0, 2, beside, across))
    cot_copies[1].append(cot_copy(1, 2, across, beside))
    for k in range(2):
        cot_copies[0][k].start()
    for k in (2, 0, 1):
        do_copies[k].start()
    swap.wait_recv()
    for k in range(2):
        cot_copies[1][k].start()

    before = jnp.where(
        plane > 0,
        seg[0:1, pl.ds(pl.multiple_of(jnp.maximum(plane * 512 - 384, 0), 128), 384)],
        -1,
    )
    here = seg[0:1, pl.ds(pl.multiple_of(plane * 512, 128), 512)]
    span = jnp.concatenate([before, here], axis=1).astype(F32)
    row_at = lax.broadcasted_iota(jnp.int32, (ROWS, 4 * ROWS), 0)
    column_at = lax.broadcasted_iota(jnp.int32, (ROWS, 4 * ROWS), 1)
    causal = column_at <= row_at + 3 * ROWS

    for k, copy in zip(range(3), (kv_copies[0], kv_copies[1], kv_copies[3])):
        copy.wait_recv()
        pass_on(ring[k])
    for k in (0, 1, 3):
        q_copies[k].wait_recv()

    scale = HEAD_DIM ** (-0.5)

    def window(block, kind):
        slots = [
            prv[index, kind] if index < 3 else own_kv[index - 3, kind]
            for index in range(block, block + 4)
        ]
        return jnp.concatenate(slots, axis=0)

    att_copy = remote(att.at[0], att.at[1], att_send, att_recv, (cp, other))

    def forward(block):
        query_segs = jnp.broadcast_to(
            span[:, (3 + block) * ROWS : (4 + block) * ROWS], (ROWS, ROWS)
        ).T
        query_segs = jnp.concatenate([query_segs] * 4, axis=1)
        visible = (span[:, block * ROWS : (block + 4) * ROWS] == query_segs) & causal
        raw = dot(own_q[block], window(block, 0), 1, 1) * scale
        scores = jnp.where(visible, raw, NEGATIVE)
        highest = jnp.max(scores, axis=1, keepdims=True)
        raised = jnp.exp(scores - highest)
        weights = raised * (1.0 / jnp.sum(raised, axis=1, keepdims=True))
        weights_of[block] = weights
        att[0, block] = dot(weights.astype(BF16), window(block, 1), 1, 0).astype(BF16)

    forward(3)
    do_copies[2].wait_recv()
    do_copies[3].start()
    for origin in range(1, XS):
        prv_copy(origin).wait_recv()
    forward(2)
    cot_copies[0][0].wait_recv()
    cot_copies[0][2].start()
    forward(1)
    cot_copies[1][1].wait_recv()
    cot_copies[1][2].start()
    forward(0)
    att_copy.start()

    def dq_copy(there):
        return remote(
            out_q.at[there],
            home_q.at[x],
            dq_send.at[there],
            dq_recv.at[x],
            (plane * XS + there, dp),
        )

    def home_copy(there):
        return remote(
            out_kv.at[there],
            home_kv.at[x],
            home_send.at[there],
            home_recv.at[x],
            (plane * XS + there, dp),
        )

    def nxt_copy(index):
        return remote(
            outn.at[index],
            nxt.at[index],
            nxt_send.at[index],
            nxt_recv.at[index],
            (plane_before * XS + x, dp),
        )

    def backward(block):
        keys = window(block, 0)
        values = window(block, 1)
        query = own_q[block]
        grad = own_do[block]
        weights = weights_of[block]
        probs = weights.astype(BF16)
        attended = att[0, block].astype(F32)
        delta = jnp.sum(grad.astype(F32) * attended, axis=1, keepdims=True)
        d_scores = (weights * (dot(grad, values, 1, 1) - delta)).astype(BF16)
        out_q[block] = (dot(d_scores, keys, 1, 0) * scale).astype(BF16)
        key_terms = dot(d_scores, query, 0, 0) * scale
        value_terms = dot(probs, grad, 0, 0)
        for part in range(4):
            index = block + part
            rows = slice(part * ROWS, (part + 1) * ROWS)
            if block == max(index - 3, 0):
                dk_acc[index] = key_terms[rows]
                dv_acc[index] = value_terms[rows]
            else:
                dk_acc[index] += key_terms[rows]
                dv_acc[index] += value_terms[rows]
        if block < 3:
            outn[block, 0] = dk_acc[block].astype(BF16)
            outn[block, 1] = dv_acc[block].astype(BF16)

    def send_home(copy, block):
        @pl.when(x != block)
        def _():
            copy(block).start()

    for k in (0, 1, 3):
        do_copies[k].wait_recv()
    backward(0)
    nxt_copy(0).start()

    cot_copies[0][1].wait_recv()
    cot_copies[1][0].wait_recv()
    for part in range(2):
        cot_copies[part][2].wait_recv()
    pl.semaphore_signal(ready, inc=1, device_id=(cp, other), device_id_type=MESH)
    att_copy.wait_recv()
    features = jnp.concatenate(
        [att[part, block] for part in range(2) for block in range(XS)], axis=0
    )
    columns = jnp.concatenate(
        [cots[block, part] for part in range(2) for block in range(XS)], axis=0
    )
    product = dot(features, columns, 0, 0)

    def exchange(at, device, parts, got, send_sem, recv_sem):
        return [
            remote(
                parts(lax.rem(at + step, 8)),
                got.at[step - 1],
                send_sem.at[step - 1],
                recv_sem.at[step - 1],
                device(step),
            )
            for step in range(1, 8)
        ]

    for pair in range(4):
        for half in range(2):
            for kind in range(2):
                first = half * 16 + kind * 8
                pieces = [
                    product[row : row + 8, pair * 128 : (pair + 1) * 128]
                    for row in range(first, 128, 32)
                ]
                part = jnp.concatenate(pieces, axis=0).astype(BF16)
                if kind == 0:
                    ya_parts[2 * pair + 1 - half] = part
                else:
                    zb_parts[pair + 4 * (x_high if half == 0 else 1 - x_high)] = part
    ya_copies = exchange(y, along_y, lambda at: ya_parts.at[at], ya_got, ya_send, ya_recv)
    zb_copies = exchange(z, along_z, lambda at: zb_parts.at[at], zb_got, zb_send, zb_recv)
    for pair in zip(ya_copies, zb_copies):
        for copy in pair:
            copy.start()

    backward(1)
    backward(2)
    for block in (1, 2):
        nxt_copy(block).start()
    pl.semaphore_wait(ready, 1)
    for block in range(3):
        send_home(dq_copy, block)

    fin_copies = []
    for kind, (copies, parts, got, at, summed) in enumerate(
        ((ya_copies, ya_parts, ya_got, y, a_sum), (zb_copies, zb_parts, zb_got, z, b_sum))
    ):
        for copy in copies:
            copy.wait_recv()
        total = parts[at].astype(F32)
        for step in range(7):
            total += got[step].astype(F32)
        summed[...] = total
        came_along = (z, y)[kind]
        for group in range(4):
            copy = remote(
                summed.at[pl.ds(8 * group, 8)],
                fin_got.at[came_along],
                fin_send.at[4 * kind + group],
                fin_recv.at[came_along],
                owners[4 * kind + group],
            )
            copy.start()
            fin_copies.append(copy)

    backward(3)
    send_home(dq_copy, 3)
    for there in range(XS):
        key_sum = dk_acc[there + 3]
        value_sum = dv_acc[there + 3]
        if there:
            nxt_copy(there - 1).wait_recv()
            key_sum += nxt[there - 1, 0].astype(F32)
            value_sum += nxt[there - 1, 1].astype(F32)
        out_kv[there, 0] = key_sum.astype(BF16)
        out_kv[there, 1] = value_sum.astype(BF16)
    for there in range(XS):
        send_home(home_copy, there)

    for step in range(1, XS):
        there = lax.rem(x + step, XS)
        for source, target, send_sem, recv_sem in (
            (out_q, home_q, dq_send, dq_recv),
            (out_kv, home_kv, home_send, home_recv),
        ):
            remote(
                source.at[0],
                target.at[there],
                send_sem.at[0],
                recv_sem.at[there],
                (along_x(step), dp),
            ).wait_recv()
    home_q[x] = out_q[x]
    home_kv[x] = out_kv[x]

    for head in range(XS):
        at = slice(head * HEAD_DIM, (head + 1) * HEAD_DIM)
        dq_out[:, at] = home_q[head].astype(F32)
        dk_out[:, at] = home_kv[head, 0].astype(F32)
        dv_out[:, at] = home_kv[head, 1].astype(F32)
    for k in range(8):
        remote(
            a_sum.at[pl.ds(0, 8)], fin_got.at[k], fin_send.at[0], fin_recv.at[k], owners[0]
        ).wait_recv()
    total = fin_got[0]
    for k in range(1, 8):
        total += fin_got[k]
    wg_out[...] = total * (1.0 / math.sqrt(ROWS * 64 * 8))

    sent = kv_copies + q_copies + do_copies + [swap, att_copy] + cot_copies[0] + cot_copies[1]
    for copy in sent + ya_copies + zb_copies + fin_copies:
        copy.wait_send()

    for origin in range(1, XS):
        prv_copy(origin).wait_send()
    for there in range(XS):

        @pl.when(x != there)
        def _(there=there):
            dq_copy(there).wait_send()
            home_copy(there).wait_send()

    for index in range(3):
        nxt_copy(index).wait_send()


def finish(*refs):
    copies = [
        pltpu.make_async_copy(refs[index], refs[4 + index], refs[8].at[index])
        for index in range(4)
    ]
    for copy in copies:
        copy.start()
    for copy in copies:
        copy.wait()


def body(queries, keys, values, segments, w_out, cotangent):
    results = [
        jax.ShapeDtypeStruct((ROWS, 512), F32),
        jax.ShapeDtypeStruct((ROWS, 512), F32),
        jax.ShapeDtypeStruct((ROWS, 512), F32),
        jax.ShapeDtypeStruct((8, 128), F32),
    ]
    dma = pltpu.SemaphoreType.DMA
    tile = (ROWS, HEAD_DIM)
    hbm = pl.BlockSpec(memory_space=pltpu.HBM)
    vmem = pl.BlockSpec(memory_space=pltpu.VMEM)
    operands = [queries[0], keys[0], values[0], segments, w_out, cotangent[0]]
    operands = [pltpu.with_memory_space_constraint(operand, pltpu.HBM) for operand in operands]
    outs = pl.pallas_call(
        kernel,
        out_shape=[pltpu.VMEM(result.shape, result.dtype) for result in results],
        in_specs=[hbm] * 6,
        out_specs=[vmem] * 4,
        scratch_shapes=[
            pltpu.VMEM((3, ROWS, 512), BF16),
            pltpu.VMEM((1, 8192), jnp.int32),
            pltpu.VMEM((512, 1024), BF16),
            pltpu.VMEM((ROWS, 1024), BF16),
            pltpu.VMEM((ROWS, 512), BF16),
            pltpu.VMEM((XS, 2, ROWS, 512), BF16),
            pltpu.VMEM((XS, 2) + tile, BF16),
            pltpu.VMEM((XS,) + tile, BF16),
            pltpu.VMEM((XS,) + tile, BF16),
            pltpu.VMEM((2,) + tile, BF16),
            pltpu.VMEM(tile, BF16),
            pltpu.VMEM(tile, BF16),
            pltpu.VMEM((XS, 2) + tile, BF16),
            pltpu.VMEM((XS,) + tile, BF16),
            pltpu.VMEM((XS,) + tile, BF16),
            pltpu.VMEM((3, 2) + tile, BF16),
            pltpu.VMEM((XS,) + tile, BF16),
            pltpu.VMEM((XS, 2) + tile, BF16),
            pltpu.VMEM((3, 2) + tile, BF16),
            pltpu.VMEM((XS,) + tile, BF16),
            pltpu.VMEM((XS, 2) + tile, BF16),
            pltpu.VMEM((3, 2) + tile, BF16),
            pltpu.VMEM((XS, ROWS, 4 * ROWS), F32),
            pltpu.VMEM((7,) + tile, F32),
            pltpu.VMEM((7,) + tile, F32),
            pltpu.VMEM((2, XS) + tile, BF16),
            pltpu.VMEM((8, 32, 128), BF16),
            pltpu.VMEM((7, 32, 128), BF16),
            pltpu.VMEM((8, 32, 128), BF16),
            pltpu.VMEM((7, 32, 128), BF16),
            pltpu.VMEM((32, 128), F32),
            pltpu.VMEM((32, 128), F32),
            pltpu.VMEM((8, 8, 128), F32),
            dma((6,)),
            dma((4,)), dma((4,)),
            dma((4,)), dma((4,)),
            dma((4,)), dma((4,)),
            dma((3,)), dma((3,)),
            dma, dma,
            dma((2, 3)), dma((2, 3)),
            dma, dma,
            dma((4,)), dma((4,)),
            dma((4,)), dma((4,)),
            dma((3,)), dma((3,)),
            dma((7,)), dma((7,)),
            dma((7,)), dma((7,)),
            dma((8,)), dma((8,)),
            pltpu.SemaphoreType.REGULAR,
        ],
        compiler_params=pltpu.CompilerParams(
            collective_id=0, has_side_effects=True, vmem_limit_bytes=32 * 1024 * 1024
        ),
        cost_estimate=pl.CostEstimate(
            flops=600_000_000, bytes_accessed=4_000_000, transcendentals=262_144
        ),
    )(*operands)
    query_grad, key_grad, value_grad, weight_grad = pl.pallas_call(
        finish,
        out_shape=results,
        in_specs=[vmem] * 4,
        out_specs=[hbm] * 4,
        scratch_shapes=[dma((4,))],
        compiler_params=pltpu.CompilerParams(vmem_limit_bytes=4 * 1024 * 1024),
        cost_estimate=pl.CostEstimate(flops=0, bytes_accessed=1_600_000, transcendentals=0),
    )(*outs)
    return (query_grad[None], key_grad[None], value_grad[None], weight_grad)


def solution(mesh):
    in_specs = (
        P("dp", "cp", None),
        P("dp", "cp", None),
        P("dp", "cp", None),
        P("dp", None),
        P(),
        P("dp", "cp", None),
    )
    out_specs = (P("dp", "cp", None), P("dp", "cp", None), P("dp", "cp", None), P("cp", "dp"))
    return jax.shard_map(body, mesh=mesh, in_specs=in_specs, out_specs=out_specs, check_vma=False)
```

```python
import math

import jax
import jax.numpy as jnp
from jax import lax
from jax.experimental import pallas as pl
from jax.experimental.pallas import tpu as pltpu
from jax.sharding import PartitionSpec as P

HEAD_DIM = 128
ROWS = 128
MESH = pl.DeviceIdType.MESH
NEGATIVE = -1e30
F32 = jnp.float32
BF16 = jnp.bfloat16

XS = 4
PLANES = 16
PEERS = 36


def dot(left, right, left_dim, right_dim):
    return lax.dot_general(
        left, right, (((left_dim,), (right_dim,)), ((), ())), preferred_element_type=F32
    )


def kernel(
    q_hbm, k_hbm, v_hbm, seg_hbm, w_hbm, cot_hbm,
    dq_out, dk_out, dv_out, wg_out,
    kvq, seg, w_out, cot, cot_other, cots, pack_kv, pack_q, pack_do,
    pass_kv, pass_q, pass_do, own_kv, own_q, own_do, prv, out_q, out_k, out_v, outn_k, outn_v,
    home_q, home_k, home_v, nxt_k, nxt_v,
    weights_of, dk_acc, dv_acc, att,
    ya_parts, ya_got, zb_parts, zb_got, a_sum, b_sum, fin_got,
    load_sem,
    kv_send, kv_recv, q_send, q_recv, do_send, do_recv, prv_send, prv_recv,
    swap_send, swap_recv, cot_send, cot_recv, att_send, att_recv,
    dq_send, dq_recv, dk_send, dk_recv, dv_send, dv_recv,
    nk_send, nk_recv, nv_send, nv_recv,
    ya_send, ya_recv, zb_send, zb_recv, fin_send, fin_recv, ready,
):
    cp = lax.axis_index("cp")
    dp = lax.axis_index("dp")
    x = lax.rem(cp, XS)
    plane = lax.div(cp, XS)
    z = lax.rem(plane, 8)
    y_lo = lax.div(plane, 8)
    core = lax.rem(dp, 2)
    other = dp + 1 - 2 * core
    y = lax.div(dp, 2) * 2 + y_lo
    plane_next = lax.rem(plane + 1, PLANES)
    plane_before = lax.rem(plane + PLANES - 1, PLANES)

    beside = x + 1 - 2 * lax.rem(x, 2)
    across = 3 - x
    opposite = lax.rem(x + 2, XS)
    x_high, z_high = lax.div(x, 2), lax.div(z, 4)
    side = (1 - z_high) * (1 - x_high) + z_high * x_high
    to_plane = x_high * 8 + lax.rem(x, 2) * 4
    owners = [((to_plane + group) * 4 + 2 * (1 - y_lo), dp) for group in range(4)]
    owners += [
        ((to_plane + group) * 4 + 2 * (1 - side) + 1, lax.rem(z, 4) * 2 + core)
        for group in range(4)
    ]
    head_from = 2 * y_lo + z_high
    z_from = lax.div(dp, 2) + 4 * ((1 - x_high) * y_lo + x_high * (1 - y_lo))
    odd_x = lax.rem(x, 2)
    summers = []
    for k in range(8):
        over_z = ((1 - x_high) * 8 + k) * 4 + head_from
        over_y = (k % 2 * 8 + z_from) * 4 + head_from
        summers.append(
            (over_z + odd_x * (over_y - over_z), dp + odd_x * (k // 2 * 2 + core - dp))
        )

    def along_x(step):
        return plane * XS + lax.rem(x + step, XS)

    def along_y(step):
        there = lax.rem(y + step, 8)
        return (lax.rem(there, 2) * 32 + z * 4 + x, lax.div(there, 2) * 2 + core)

    def along_z(step):
        return ((y_lo * 8 + lax.rem(z + step, 8)) * 4 + x, dp)

    def remote(source, target, send_sem, recv_sem, device):
        return pltpu.make_async_remote_copy(
            src_ref=source,
            dst_ref=target,
            send_sem=send_sem,
            recv_sem=recv_sem,
            device_id=device,
            device_id_type=MESH,
        )

    loads = [
        pltpu.make_async_copy(k_hbm, kvq.at[0], load_sem.at[0]),
        pltpu.make_async_copy(v_hbm, kvq.at[1], load_sem.at[1]),
        pltpu.make_async_copy(q_hbm, kvq.at[2], load_sem.at[2]),
        pltpu.make_async_copy(cot_hbm, cot, load_sem.at[3]),
        pltpu.make_async_copy(w_hbm, w_out, load_sem.at[4]),
        pltpu.make_async_copy(seg_hbm, seg, load_sem.at[5]),
    ]
    for load in loads:
        load.start()

    barrier = pltpu.get_barrier_semaphore()
    peers = [(along_x(step), dp) for step in range(1, XS)]
    peers += [(cp, other)] + owners + summers
    peers += [(plane_next * XS + x, dp), (plane_before * XS + x, dp)]
    peers += [along_y(step) for step in range(1, 8)]
    peers += [along_z(step) for step in range(1, 8)]
    for peer in peers:
        pl.semaphore_signal(barrier, inc=1, device_id=peer, device_id_type=MESH)

    for load in loads[:3]:
        load.wait()
    for head in range(XS):
        at = slice(head * HEAD_DIM, (head + 1) * HEAD_DIM)
        pack_kv[head, 0] = kvq[0, :, at]
        pack_kv[head, 1] = kvq[1, :, at]
        pack_q[head] = kvq[2, :, at]

    pl.semaphore_wait(barrier, PEERS)

    ring = {0: beside, 1: across, 2: opposite}

    def at_x(there):
        return (plane * XS + there, dp)

    def to_ring(pack, passing, own, send_sem, recv_sem):
        direct = [
            remote(pack.at[ring[k]], own.at[x], send_sem.at[k], recv_sem.at[k], at_x(ring[k]))
            for k in range(2)
        ]
        first = remote(pack.at[opposite], passing, send_sem.at[2], recv_sem.at[2], at_x(beside))
        second = remote(passing, own.at[beside], send_sem.at[3], recv_sem.at[3], at_x(across))
        return direct + [first, second]

    kv_copies = to_ring(pack_kv, pass_kv, own_kv, kv_send, kv_recv)
    q_copies = to_ring(pack_q, pass_q, own_q, q_send, q_recv)
    do_copies = to_ring(pack_do, pass_do, own_do, do_send, do_recv)
    for copies in (kv_copies, q_copies):
        for k in (2, 0, 1):
            copies[k].start()
    own_kv[x] = pack_kv[x]
    own_q[x] = pack_q[x]

    def prv_copy(origin):
        return remote(
            own_kv.at[origin],
            prv.at[origin - 1],
            prv_send.at[origin - 1],
            prv_recv.at[origin - 1],
            (plane_next * XS + x, dp),
        )

    def pass_on(origin):
        @pl.when(origin > 0)
        def _():
            prv_copy(origin).start()

    pass_on(x)

    loads[3].wait()
    for pair in range(4):
        at = slice(pair * 128, (pair + 1) * 128)
        even = cot[:, pair * 256 : pair * 256 + 128]
        odd = cot[:, pair * 256 + 128 : (pair + 1) * 256]
        cots[x, 0, :, at] = jnp.where(core == 0, even, odd)
        cot_other[:, at] = jnp.where(core == 0, odd, even)
    swap = remote(cot_other, cots.at[x, 1], swap_send, swap_recv, (cp, other))
    swap.start()

    for load in loads[4:]:
        load.wait()
    grads = dot(cot[...], w_out[...], 1, 1).astype(BF16)
    for head in range(XS):
        pack_do[head] = grads[:, head * HEAD_DIM : (head + 1) * HEAD_DIM]
    own_do[x] = pack_do[x]

    for copies in (kv_copies, q_copies):
        copies[2].wait_recv()
        copies[3].start()

    def cot_copy(part, kind, origin, target):
        return remote(
            cots.at[origin, part],
            cots.at[origin, part],
            cot_send.at[part, kind],
            cot_recv.at[part, kind],
            at_x(target),
        )

    cot_copies = [
        [cot_copy(part, 0, x, beside), cot_copy(part, 1, x, across)] for part in range(2)
    ]
    cot_copies[0].append(cot_copy(0, 2, beside, across))
    cot_copies[1].append(cot_copy(1, 2, across, beside))
    for k in range(2):
        cot_copies[0][k].start()
    for k in (2, 0, 1):
        do_copies[k].start()
    swap.wait_recv()
    for k in range(2):
        cot_copies[1][k].start()

    before = jnp.where(
        plane > 0,
        seg[0:1, pl.ds(pl.multiple_of(jnp.maximum(plane * 512 - 384, 0), 128), 384)],
        -1,
    )
    here = seg[0:1, pl.ds(pl.multiple_of(plane * 512, 128), 512)]
    span = jnp.concatenate([before, here], axis=1).astype(F32)
    row_at = lax.broadcasted_iota(jnp.int32, (ROWS, 4 * ROWS), 0)
    column_at = lax.broadcasted_iota(jnp.int32, (ROWS, 4 * ROWS), 1)
    causal = column_at <= row_at + 3 * ROWS

    for k, copy in zip(range(3), (kv_copies[0], kv_copies[1], kv_copies[3])):
        copy.wait_recv()
        pass_on(ring[k])
    for k in (0, 1, 3):
        q_copies[k].wait_recv()

    scale = HEAD_DIM ** (-0.5)

    def window(block, kind):
        slots = [
            prv[index, kind] if index < 3 else own_kv[index - 3, kind]
            for index in range(block, block + 4)
        ]
        return jnp.concatenate(slots, axis=0)

    att_copy = remote(att.at[0], att.at[1], att_send, att_recv, (cp, other))

    def forward(block):
        query_segs = jnp.broadcast_to(
            span[:, (3 + block) * ROWS : (4 + block) * ROWS], (ROWS, ROWS)
        ).T
        query_segs = jnp.concatenate([query_segs] * 4, axis=1)
        visible = (span[:, block * ROWS : (block + 4) * ROWS] == query_segs) & causal
        raw = dot(own_q[block], window(block, 0), 1, 1) * scale
        scores = jnp.where(visible, raw, NEGATIVE)
        highest = jnp.max(scores, axis=1, keepdims=True)
        raised = jnp.exp(scores - highest)
        weights = raised * (1.0 / jnp.sum(raised, axis=1, keepdims=True))
        weights_of[block] = weights
        att[0, block] = dot(weights.astype(BF16), window(block, 1), 1, 0).astype(BF16)

    forward(3)
    do_copies[2].wait_recv()
    do_copies[3].start()
    for origin in range(1, XS):
        prv_copy(origin).wait_recv()
    for block in (2, 1, 0):
        forward(block)
    att_copy.start()

    cot_copies[0][0].wait_recv()
    cot_copies[0][2].start()
    cot_copies[1][1].wait_recv()
    cot_copies[1][2].start()

    def to_home(out, home, send_sem, recv_sem):
        return [
            remote(
                out.at[there],
                home.at[x],
                send_sem.at[there],
                recv_sem.at[x],
                (plane * XS + there, dp),
            )
            for there in range(XS)
        ]

    dq_copies = to_home(out_q, home_q, dq_send, dq_recv)
    dk_copies = to_home(out_k, home_k, dk_send, dk_recv)
    dv_copies = to_home(out_v, home_v, dv_send, dv_recv)

    nk_copy = remote(outn_k, nxt_k, nk_send, nk_recv, (plane_before * XS + x, dp))
    nv_copy = remote(outn_v, nxt_v, nv_send, nv_recv, (plane_before * XS + x, dp))

    def accumulate(total_ref, block, terms):
        for part in range(4):
            index = block + part
            rows = slice(part * ROWS, (part + 1) * ROWS)
            if block == max(index - 3, 0):
                total_ref[index] = terms[rows]
            else:
                total_ref[index] += terms[rows]

    def add_next(total_ref, nxt, out):
        for there in range(XS):
            total = total_ref[there + 3]
            if there:
                total += nxt[there - 1].astype(F32)
            out[there] = total.astype(BF16)

    def backward(block):
        keys = window(block, 0)
        values = window(block, 1)
        query = own_q[block]
        grad = own_do[block]
        weights = weights_of[block]
        attended = att[0, block].astype(F32)
        delta = jnp.sum(grad.astype(F32) * attended, axis=1, keepdims=True)
        d_scores = (weights * (dot(grad, values, 1, 1) - delta)).astype(BF16)
        out_q[block] = (dot(d_scores, keys, 1, 0) * scale).astype(BF16)
        accumulate(dk_acc, block, dot(d_scores, query, 0, 0) * scale)

    def send_home(copies, block):
        @pl.when(x != block)
        def _():
            copies[block].start()

    for k in (0, 1, 3):
        do_copies[k].wait_recv()
    for block in range(XS):
        accumulate(dv_acc, block, dot(weights_of[block].astype(BF16), own_do[block], 0, 0))
    for index in range(3):
        outn_v[index] = dv_acc[index].astype(BF16)
    nv_copy.start()

    cot_copies[0][1].wait_recv()
    cot_copies[1][0].wait_recv()
    for part in range(2):
        cot_copies[part][2].wait_recv()
    pl.semaphore_signal(ready, inc=1, device_id=(cp, other), device_id_type=MESH)
    att_copy.wait_recv()
    features = jnp.concatenate(
        [att[part, block] for part in range(2) for block in range(XS)], axis=0
    )
    columns = jnp.concatenate(
        [cots[block, part] for part in range(2) for block in range(XS)], axis=0
    )
    product = dot(features, columns, 0, 0)

    def exchange(at, device, parts, got, send_sem, recv_sem):
        return [
            remote(
                parts(lax.rem(at + step, 8)),
                got.at[step - 1],
                send_sem.at[step - 1],
                recv_sem.at[step - 1],
                device(step),
            )
            for step in range(1, 8)
        ]

    for pair in range(4):
        for half in range(2):
            for kind in range(2):
                first = half * 16 + kind * 8
                pieces = [
                    product[row : row + 8, pair * 128 : (pair + 1) * 128]
                    for row in range(first, 128, 32)
                ]
                part = jnp.concatenate(pieces, axis=0).astype(BF16)
                if kind == 0:
                    ya_parts[2 * pair + 1 - half] = part
                else:
                    zb_parts[pair + 4 * (x_high if half == 0 else 1 - x_high)] = part
    ya_copies = exchange(y, along_y, lambda at: ya_parts.at[at], ya_got, ya_send, ya_recv)
    zb_copies = exchange(z, along_z, lambda at: zb_parts.at[at], zb_got, zb_send, zb_recv)
    for pair in zip(ya_copies, zb_copies):
        for copy in pair:
            copy.start()

    for block in range(3):
        backward(block)
    for index in range(3):
        outn_k[index] = dk_acc[index].astype(BF16)
    nk_copy.start()
    nv_copy.wait_recv()
    add_next(dv_acc, nxt_v, out_v)
    pl.semaphore_wait(ready, 1)
    for block in range(3):
        send_home(dq_copies, block)
    for block in range(XS):
        send_home(dv_copies, block)

    fin_copies = []
    for kind, (copies, parts, got, at, summed) in enumerate(
        ((ya_copies, ya_parts, ya_got, y, a_sum), (zb_copies, zb_parts, zb_got, z, b_sum))
    ):
        for copy in copies:
            copy.wait_recv()
        total = parts[at].astype(F32)
        for step in range(7):
            total += got[step].astype(F32)
        summed[...] = total
        came_along = (z, y)[kind]
        for group in range(4):
            copy = remote(
                summed.at[pl.ds(8 * group, 8)],
                fin_got.at[came_along],
                fin_send.at[4 * kind + group],
                fin_recv.at[came_along],
                owners[4 * kind + group],
            )
            copy.start()
            fin_copies.append(copy)

    backward(3)
    send_home(dq_copies, 3)
    nk_copy.wait_recv()
    add_next(dk_acc, nxt_k, out_k)
    for there in range(XS):
        send_home(dk_copies, there)

    for step in range(1, XS):
        there = lax.rem(x + step, XS)
        for source, target, send_sem, recv_sem in (
            (out_q, home_q, dq_send, dq_recv),
            (out_k, home_k, dk_send, dk_recv),
            (out_v, home_v, dv_send, dv_recv),
        ):
            remote(
                source.at[0],
                target.at[there],
                send_sem.at[0],
                recv_sem.at[there],
                (along_x(step), dp),
            ).wait_recv()
    home_q[x] = out_q[x]
    home_k[x] = out_k[x]
    home_v[x] = out_v[x]

    for head in range(XS):
        at = slice(head * HEAD_DIM, (head + 1) * HEAD_DIM)
        dq_out[:, at] = home_q[head].astype(F32)
        dk_out[:, at] = home_k[head].astype(F32)
        dv_out[:, at] = home_v[head].astype(F32)
    for k in range(8):
        remote(
            a_sum.at[pl.ds(0, 8)], fin_got.at[k], fin_send.at[0], fin_recv.at[k], owners[0]
        ).wait_recv()
    total = fin_got[0]
    for k in range(1, 8):
        total += fin_got[k]
    wg_out[...] = total * (1.0 / math.sqrt(ROWS * 64 * 8))

    sent = kv_copies + q_copies + do_copies + [swap, att_copy] + cot_copies[0] + cot_copies[1]
    for copy in sent + ya_copies + zb_copies + fin_copies:
        copy.wait_send()

    for origin in range(1, XS):
        prv_copy(origin).wait_send()
    for there in range(XS):

        @pl.when(x != there)
        def _(there=there):
            for copies in (dq_copies, dk_copies, dv_copies):
                copies[there].wait_send()

    nk_copy.wait_send()
    nv_copy.wait_send()


def finish(*refs):
    copies = [
        pltpu.make_async_copy(refs[index], refs[4 + index], refs[8].at[index])
        for index in range(4)
    ]
    for copy in copies:
        copy.start()
    for copy in copies:
        copy.wait()


def body(queries, keys, values, segments, w_out, cotangent):
    results = [
        jax.ShapeDtypeStruct((ROWS, 512), F32),
        jax.ShapeDtypeStruct((ROWS, 512), F32),
        jax.ShapeDtypeStruct((ROWS, 512), F32),
        jax.ShapeDtypeStruct((8, 128), F32),
    ]
    dma = pltpu.SemaphoreType.DMA
    tile = (ROWS, HEAD_DIM)
    hbm = pl.BlockSpec(memory_space=pltpu.HBM)
    vmem = pl.BlockSpec(memory_space=pltpu.VMEM)
    operands = [queries[0], keys[0], values[0], segments, w_out, cotangent[0]]
    operands = [pltpu.with_memory_space_constraint(operand, pltpu.HBM) for operand in operands]
    outs = pl.pallas_call(
        kernel,
        out_shape=[pltpu.VMEM(result.shape, result.dtype) for result in results],
        in_specs=[hbm] * 6,
        out_specs=[vmem] * 4,
        scratch_shapes=[
            pltpu.VMEM((3, ROWS, 512), BF16),
            pltpu.VMEM((1, 8192), jnp.int32),
            pltpu.VMEM((512, 1024), BF16),
            pltpu.VMEM((ROWS, 1024), BF16),
            pltpu.VMEM((ROWS, 512), BF16),
            pltpu.VMEM((XS, 2, ROWS, 512), BF16),
            pltpu.VMEM((XS, 2) + tile, BF16),
            pltpu.VMEM((XS,) + tile, BF16),
            pltpu.VMEM((XS,) + tile, BF16),
            pltpu.VMEM((2,) + tile, BF16),
            pltpu.VMEM(tile, BF16),
            pltpu.VMEM(tile, BF16),
            pltpu.VMEM((XS, 2) + tile, BF16),
            pltpu.VMEM((XS,) + tile, BF16),
            pltpu.VMEM((XS,) + tile, BF16),
            pltpu.VMEM((3, 2) + tile, BF16),
            pltpu.VMEM((XS,) + tile, BF16),
            pltpu.VMEM((XS,) + tile, BF16),
            pltpu.VMEM((XS,) + tile, BF16),
            pltpu.VMEM((3,) + tile, BF16),
            pltpu.VMEM((3,) + tile, BF16),
            pltpu.VMEM((XS,) + tile, BF16),
            pltpu.VMEM((XS,) + tile, BF16),
            pltpu.VMEM((XS,) + tile, BF16),
            pltpu.VMEM((3,) + tile, BF16),
            pltpu.VMEM((3,) + tile, BF16),
            pltpu.VMEM((XS, ROWS, 4 * ROWS), F32),
            pltpu.VMEM((7,) + tile, F32),
            pltpu.VMEM((7,) + tile, F32),
            pltpu.VMEM((2, XS) + tile, BF16),
            pltpu.VMEM((8, 32, 128), BF16),
            pltpu.VMEM((7, 32, 128), BF16),
            pltpu.VMEM((8, 32, 128), BF16),
            pltpu.VMEM((7, 32, 128), BF16),
            pltpu.VMEM((32, 128), F32),
            pltpu.VMEM((32, 128), F32),
            pltpu.VMEM((8, 8, 128), F32),
            dma((6,)),
            dma((4,)), dma((4,)),
            dma((4,)), dma((4,)),
            dma((4,)), dma((4,)),
            dma((3,)), dma((3,)),
            dma, dma,
            dma((2, 3)), dma((2, 3)),
            dma, dma,
            dma((4,)), dma((4,)),
            dma((4,)), dma((4,)),
            dma((4,)), dma((4,)),
            dma, dma,
            dma, dma,
            dma((7,)), dma((7,)),
            dma((7,)), dma((7,)),
            dma((8,)), dma((8,)),
            pltpu.SemaphoreType.REGULAR,
        ],
        compiler_params=pltpu.CompilerParams(
            collective_id=0, has_side_effects=True, vmem_limit_bytes=32 * 1024 * 1024
        ),
        cost_estimate=pl.CostEstimate(
            flops=600_000_000, bytes_accessed=4_000_000, transcendentals=262_144
        ),
    )(*operands)
    query_grad, key_grad, value_grad, weight_grad = pl.pallas_call(
        finish,
        out_shape=results,
        in_specs=[vmem] * 4,
        out_specs=[hbm] * 4,
        scratch_shapes=[dma((4,))],
        compiler_params=pltpu.CompilerParams(vmem_limit_bytes=4 * 1024 * 1024),
        cost_estimate=pl.CostEstimate(flops=0, bytes_accessed=1_600_000, transcendentals=0),
    )(*outs)
    return (query_grad[None], key_grad[None], value_grad[None], weight_grad)


def solution(mesh):
    in_specs = (
        P("dp", "cp", None),
        P("dp", "cp", None),
        P("dp", "cp", None),
        P("dp", None),
        P(),
        P("dp", "cp", None),
    )
    out_specs = (P("dp", "cp", None), P("dp", "cp", None), P("dp", "cp", None), P("cp", "dp"))
    return jax.shard_map(body, mesh=mesh, in_specs=in_specs, out_specs=out_specs, check_vma=False)
```

```python
import math

import jax
import jax.numpy as jnp
from jax import lax
from jax.experimental import pallas as pl
from jax.experimental.pallas import tpu as pltpu
from jax.sharding import PartitionSpec as P

HEAD_DIM = 128
ROWS = 128
MESH = pl.DeviceIdType.MESH
NEGATIVE = -1e30
F32 = jnp.float32
BF16 = jnp.bfloat16

XS = 4
PLANES = 16
PEERS = 36


def dot(left, right, left_dim, right_dim):
    return lax.dot_general(
        left, right, (((left_dim,), (right_dim,)), ((), ())), preferred_element_type=F32
    )


def kernel(
    q_hbm, k_hbm, v_hbm, seg_hbm, w_hbm, cot_hbm,
    dq_out, dk_out, dv_out, wg_out,
    kvq, seg, w_out, cot, cot_other, cots, pack_kv, pack_q, pack_do,
    pass_kv, pass_q, pass_do, own_kv, own_q, own_do, prv, out_q, out_kv, outn, home_q, home_kv, nxt,
    weights_of, dk_acc, dv_acc, att,
    ya_parts, ya_got, zb_parts, zb_got, a_sum, b_sum, fin_got,
    load_sem,
    kv_send, kv_recv, q_send, q_recv, do_send, do_recv, prv_send, prv_recv,
    swap_send, swap_recv, cot_send, cot_recv, att_send, att_recv,
    dq_send, dq_recv, home_send, home_recv, nxt_send, nxt_recv,
    ya_send, ya_recv, zb_send, zb_recv, fin_send, fin_recv, ready,
):
    cp = lax.axis_index("cp")
    dp = lax.axis_index("dp")
    x = lax.rem(cp, XS)
    plane = lax.div(cp, XS)
    z = lax.rem(plane, 8)
    y_lo = lax.div(plane, 8)
    core = lax.rem(dp, 2)
    other = dp + 1 - 2 * core
    y = lax.div(dp, 2) * 2 + y_lo
    plane_next = lax.rem(plane + 1, PLANES)
    plane_before = lax.rem(plane + PLANES - 1, PLANES)

    beside = x + 1 - 2 * lax.rem(x, 2)
    across = 3 - x
    opposite = lax.rem(x + 2, XS)
    x_high, z_high = lax.div(x, 2), lax.div(z, 4)
    side = (1 - z_high) * (1 - x_high) + z_high * x_high
    to_plane = x_high * 8 + lax.rem(x, 2) * 4
    owners = [((to_plane + group) * 4 + 2 * (1 - y_lo), dp) for group in range(4)]
    owners += [
        ((to_plane + group) * 4 + 2 * (1 - side) + 1, lax.rem(z, 4) * 2 + core)
        for group in range(4)
    ]
    head_from = 2 * y_lo + z_high
    z_from = lax.div(dp, 2) + 4 * ((1 - x_high) * y_lo + x_high * (1 - y_lo))
    odd_x = lax.rem(x, 2)
    summers = []
    for k in range(8):
        over_z = ((1 - x_high) * 8 + k) * 4 + head_from
        over_y = (k % 2 * 8 + z_from) * 4 + head_from
        summers.append(
            (over_z + odd_x * (over_y - over_z), dp + odd_x * (k // 2 * 2 + core - dp))
        )

    def along_x(step):
        return plane * XS + lax.rem(x + step, XS)

    def along_y(step):
        there = lax.rem(y + step, 8)
        return (lax.rem(there, 2) * 32 + z * 4 + x, lax.div(there, 2) * 2 + core)

    def along_z(step):
        return ((y_lo * 8 + lax.rem(z + step, 8)) * 4 + x, dp)

    def remote(source, target, send_sem, recv_sem, device):
        return pltpu.make_async_remote_copy(
            src_ref=source,
            dst_ref=target,
            send_sem=send_sem,
            recv_sem=recv_sem,
            device_id=device,
            device_id_type=MESH,
        )

    loads = [
        pltpu.make_async_copy(k_hbm, kvq.at[0], load_sem.at[0]),
        pltpu.make_async_copy(v_hbm, kvq.at[1], load_sem.at[1]),
        pltpu.make_async_copy(q_hbm, kvq.at[2], load_sem.at[2]),
        pltpu.make_async_copy(cot_hbm, cot, load_sem.at[3]),
        pltpu.make_async_copy(w_hbm, w_out, load_sem.at[4]),
        pltpu.make_async_copy(seg_hbm, seg, load_sem.at[5]),
    ]
    for load in loads:
        load.start()

    barrier = pltpu.get_barrier_semaphore()
    peers = [(along_x(step), dp) for step in range(1, XS)]
    peers += [(cp, other)] + owners + summers
    peers += [(plane_next * XS + x, dp), (plane_before * XS + x, dp)]
    peers += [along_y(step) for step in range(1, 8)]
    peers += [along_z(step) for step in range(1, 8)]
    for peer in peers:
        pl.semaphore_signal(barrier, inc=1, device_id=peer, device_id_type=MESH)

    for load in loads[:3]:
        load.wait()
    for head in range(XS):
        at = slice(head * HEAD_DIM, (head + 1) * HEAD_DIM)
        pack_kv[head, 0] = kvq[0, :, at]
        pack_kv[head, 1] = kvq[1, :, at]
        pack_q[head] = kvq[2, :, at]

    pl.semaphore_wait(barrier, PEERS)

    ring = {0: beside, 1: across, 2: opposite}

    def at_x(there):
        return (plane * XS + there, dp)

    def to_ring(pack, passing, own, send_sem, recv_sem):
        direct = [
            remote(pack.at[ring[k]], own.at[x], send_sem.at[k], recv_sem.at[k], at_x(ring[k]))
            for k in range(2)
        ]
        first = remote(pack.at[opposite], passing, send_sem.at[2], recv_sem.at[2], at_x(beside))
        second = remote(passing, own.at[beside], send_sem.at[3], recv_sem.at[3], at_x(across))
        return direct + [first, second]

    kv_copies = to_ring(pack_kv, pass_kv, own_kv, kv_send, kv_recv)
    q_copies = to_ring(pack_q, pass_q, own_q, q_send, q_recv)
    do_copies = to_ring(pack_do, pass_do, own_do, do_send, do_recv)
    for copies in (kv_copies, q_copies):
        for k in (2, 0, 1):
            copies[k].start()
    own_kv[x] = pack_kv[x]
    own_q[x] = pack_q[x]

    def prv_copy(origin):
        return remote(
            own_kv.at[origin],
            prv.at[origin - 1],
            prv_send.at[origin - 1],
            prv_recv.at[origin - 1],
            (plane_next * XS + x, dp),
        )

    def pass_on(origin):
        @pl.when(origin > 0)
        def _():
            prv_copy(origin).start()

    pass_on(x)

    loads[3].wait()
    for pair in range(4):
        at = slice(pair * 128, (pair + 1) * 128)
        even = cot[:, pair * 256 : pair * 256 + 128]
        odd = cot[:, pair * 256 + 128 : (pair + 1) * 256]
        cots[x, 0, :, at] = jnp.where(core == 0, even, odd)
        cot_other[:, at] = jnp.where(core == 0, odd, even)
    swap = remote(cot_other, cots.at[x, 1], swap_send, swap_recv, (cp, other))
    swap.start()

    for load in loads[4:]:
        load.wait()
    grads = dot(cot[...], w_out[...], 1, 1).astype(BF16)
    for head in range(XS):
        pack_do[head] = grads[:, head * HEAD_DIM : (head + 1) * HEAD_DIM]
    own_do[x] = pack_do[x]

    for copies in (kv_copies, q_copies):
        copies[2].wait_recv()
        copies[3].start()

    def cot_copy(part, kind, origin, target):
        return remote(
            cots.at[origin, part],
            cots.at[origin, part],
            cot_send.at[part, kind],
            cot_recv.at[part, kind],
            at_x(target),
        )

    cot_copies = [
        [cot_copy(part, 0, x, beside), cot_copy(part, 1, x, across)] for part in range(2)
    ]
    cot_copies[0].append(cot_copy(0, 2, beside, across))
    cot_copies[1].append(cot_copy(1, 2, across, beside))
    for k in range(2):
        cot_copies[0][k].start()
    swap.wait_recv()
    for k in range(2):
        cot_copies[1][k].start()
    for k in (2, 0, 1):
        do_copies[k].start()

    before = jnp.where(
        plane > 0,
        seg[0:1, pl.ds(pl.multiple_of(jnp.maximum(plane * 512 - 384, 0), 128), 384)],
        -1,
    )
    here = seg[0:1, pl.ds(pl.multiple_of(plane * 512, 128), 512)]
    span = jnp.concatenate([before, here], axis=1).astype(F32)
    row_at = lax.broadcasted_iota(jnp.int32, (ROWS, 4 * ROWS), 0)
    column_at = lax.broadcasted_iota(jnp.int32, (ROWS, 4 * ROWS), 1)
    causal = column_at <= row_at + 3 * ROWS

    for k, copy in zip(range(3), (kv_copies[0], kv_copies[1], kv_copies[3])):
        copy.wait_recv()
        pass_on(ring[k])
    for k in (0, 1, 3):
        q_copies[k].wait_recv()

    scale = HEAD_DIM ** (-0.5)

    def window(block, kind):
        slots = [
            prv[index, kind] if index < 3 else own_kv[index - 3, kind]
            for index in range(block, block + 4)
        ]
        return jnp.concatenate(slots, axis=0)

    att_copy = remote(att.at[0], att.at[1], att_send, att_recv, (cp, other))

    def forward(block):
        query_segs = jnp.broadcast_to(
            span[:, (3 + block) * ROWS : (4 + block) * ROWS], (ROWS, ROWS)
        ).T
        query_segs = jnp.concatenate([query_segs] * 4, axis=1)
        visible = (span[:, block * ROWS : (block + 4) * ROWS] == query_segs) & causal
        raw = dot(own_q[block], window(block, 0), 1, 1) * scale
        scores = jnp.where(visible, raw, NEGATIVE)
        highest = jnp.max(scores, axis=1, keepdims=True)
        raised = jnp.exp(scores - highest)
        weights = raised * (1.0 / jnp.sum(raised, axis=1, keepdims=True))
        weights_of[block] = weights
        att[0, block] = dot(weights.astype(BF16), window(block, 1), 1, 0).astype(BF16)

    forward(3)
    for origin in range(1, XS):
        prv_copy(origin).wait_recv()
    for block in (2, 1, 0):
        forward(block)
    att_copy.start()
    do_copies[2].wait_recv()
    do_copies[3].start()

    cot_copies[0][0].wait_recv()
    cot_copies[0][2].start()
    cot_copies[1][1].wait_recv()
    cot_copies[1][2].start()

    def dq_copy(there):
        return remote(
            out_q.at[there],
            home_q.at[x],
            dq_send.at[there],
            dq_recv.at[x],
            (plane * XS + there, dp),
        )

    def home_copy(there):
        return remote(
            out_kv.at[there],
            home_kv.at[x],
            home_send.at[there],
            home_recv.at[x],
            (plane * XS + there, dp),
        )

    def nxt_copy(index):
        return remote(
            outn.at[index],
            nxt.at[index],
            nxt_send.at[index],
            nxt_recv.at[index],
            (plane_before * XS + x, dp),
        )

    def backward(block):
        keys = window(block, 0)
        values = window(block, 1)
        query = own_q[block]
        grad = own_do[block]
        weights = weights_of[block]
        probs = weights.astype(BF16)
        attended = att[0, block].astype(F32)
        delta = jnp.sum(grad.astype(F32) * attended, axis=1, keepdims=True)
        d_scores = (weights * (dot(grad, values, 1, 1) - delta)).astype(BF16)
        out_q[block] = (dot(d_scores, keys, 1, 0) * scale).astype(BF16)
        key_terms = dot(d_scores, query, 0, 0) * scale
        value_terms = dot(probs, grad, 0, 0)
        for part in range(4):
            index = block + part
            rows = slice(part * ROWS, (part + 1) * ROWS)
            if block == max(index - 3, 0):
                dk_acc[index] = key_terms[rows]
                dv_acc[index] = value_terms[rows]
            else:
                dk_acc[index] += key_terms[rows]
                dv_acc[index] += value_terms[rows]
        if block < 3:
            outn[block, 0] = dk_acc[block].astype(BF16)
            outn[block, 1] = dv_acc[block].astype(BF16)

    def send_home(copy, block):
        @pl.when(x != block)
        def _():
            copy(block).start()


    cot_copies[0][1].wait_recv()
    cot_copies[1][0].wait_recv()
    for part in range(2):
        cot_copies[part][2].wait_recv()
    pl.semaphore_signal(ready, inc=1, device_id=(cp, other), device_id_type=MESH)
    att_copy.wait_recv()
    features = jnp.concatenate(
        [att[part, block] for part in range(2) for block in range(XS)], axis=0
    )
    columns = jnp.concatenate(
        [cots[block, part] for part in range(2) for block in range(XS)], axis=0
    )
    product = dot(features, columns, 0, 0)

    def exchange(at, device, parts, got, send_sem, recv_sem):
        return [
            remote(
                parts(lax.rem(at + step, 8)),
                got.at[step - 1],
                send_sem.at[step - 1],
                recv_sem.at[step - 1],
                device(step),
            )
            for step in range(1, 8)
        ]

    for pair in range(4):
        for half in range(2):
            for kind in range(2):
                first = half * 16 + kind * 8
                pieces = [
                    product[row : row + 8, pair * 128 : (pair + 1) * 128]
                    for row in range(first, 128, 32)
                ]
                part = jnp.concatenate(pieces, axis=0).astype(BF16)
                if kind == 0:
                    ya_parts[2 * pair + 1 - half] = part
                else:
                    zb_parts[pair + 4 * (x_high if half == 0 else 1 - x_high)] = part
    ya_copies = exchange(y, along_y, lambda at: ya_parts.at[at], ya_got, ya_send, ya_recv)
    zb_copies = exchange(z, along_z, lambda at: zb_parts.at[at], zb_got, zb_send, zb_recv)
    for pair in zip(ya_copies, zb_copies):
        for copy in pair:
            copy.start()

    for k in (0, 1, 3):
        do_copies[k].wait_recv()
    backward(0)
    nxt_copy(0).start()
    backward(1)
    backward(2)
    for block in (1, 2):
        nxt_copy(block).start()
    pl.semaphore_wait(ready, 1)
    for block in range(3):
        send_home(dq_copy, block)

    fin_copies = []
    for kind, (copies, parts, got, at, summed) in enumerate(
        ((ya_copies, ya_parts, ya_got, y, a_sum), (zb_copies, zb_parts, zb_got, z, b_sum))
    ):
        for copy in copies:
            copy.wait_recv()
        total = parts[at].astype(F32)
        for step in range(7):
            total += got[step].astype(F32)
        summed[...] = total
        came_along = (z, y)[kind]
        for group in range(4):
            copy = remote(
                summed.at[pl.ds(8 * group, 8)],
                fin_got.at[came_along],
                fin_send.at[4 * kind + group],
                fin_recv.at[came_along],
                owners[4 * kind + group],
            )
            copy.start()
            fin_copies.append(copy)

    backward(3)
    send_home(dq_copy, 3)
    for there in range(XS):
        key_sum = dk_acc[there + 3]
        value_sum = dv_acc[there + 3]
        if there:
            nxt_copy(there - 1).wait_recv()
            key_sum += nxt[there - 1, 0].astype(F32)
            value_sum += nxt[there - 1, 1].astype(F32)
        out_kv[there, 0] = key_sum.astype(BF16)
        out_kv[there, 1] = value_sum.astype(BF16)
    for there in range(XS):
        send_home(home_copy, there)

    for step in range(1, XS):
        there = lax.rem(x + step, XS)
        for source, target, send_sem, recv_sem in (
            (out_q, home_q, dq_send, dq_recv),
            (out_kv, home_kv, home_send, home_recv),
        ):
            remote(
                source.at[0],
                target.at[there],
                send_sem.at[0],
                recv_sem.at[there],
                (along_x(step), dp),
            ).wait_recv()
    home_q[x] = out_q[x]
    home_kv[x] = out_kv[x]

    for head in range(XS):
        at = slice(head * HEAD_DIM, (head + 1) * HEAD_DIM)
        dq_out[:, at] = home_q[head].astype(F32)
        dk_out[:, at] = home_kv[head, 0].astype(F32)
        dv_out[:, at] = home_kv[head, 1].astype(F32)
    for k in range(8):
        remote(
            a_sum.at[pl.ds(0, 8)], fin_got.at[k], fin_send.at[0], fin_recv.at[k], owners[0]
        ).wait_recv()
    total = fin_got[0]
    for k in range(1, 8):
        total += fin_got[k]
    wg_out[...] = total * (1.0 / math.sqrt(ROWS * 64 * 8))

    sent = kv_copies + q_copies + do_copies + [swap, att_copy] + cot_copies[0] + cot_copies[1]
    for copy in sent + ya_copies + zb_copies + fin_copies:
        copy.wait_send()

    for origin in range(1, XS):
        prv_copy(origin).wait_send()
    for there in range(XS):

        @pl.when(x != there)
        def _(there=there):
            dq_copy(there).wait_send()
            home_copy(there).wait_send()

    for index in range(3):
        nxt_copy(index).wait_send()


def finish(*refs):
    copies = [
        pltpu.make_async_copy(refs[index], refs[4 + index], refs[8].at[index])
        for index in range(4)
    ]
    for copy in copies:
        copy.start()
    for copy in copies:
        copy.wait()


def body(queries, keys, values, segments, w_out, cotangent):
    results = [
        jax.ShapeDtypeStruct((ROWS, 512), F32),
        jax.ShapeDtypeStruct((ROWS, 512), F32),
        jax.ShapeDtypeStruct((ROWS, 512), F32),
        jax.ShapeDtypeStruct((8, 128), F32),
    ]
    dma = pltpu.SemaphoreType.DMA
    tile = (ROWS, HEAD_DIM)
    hbm = pl.BlockSpec(memory_space=pltpu.HBM)
    vmem = pl.BlockSpec(memory_space=pltpu.VMEM)
    operands = [queries[0], keys[0], values[0], segments, w_out, cotangent[0]]
    operands = [pltpu.with_memory_space_constraint(operand, pltpu.HBM) for operand in operands]
    outs = pl.pallas_call(
        kernel,
        out_shape=[pltpu.VMEM(result.shape, result.dtype) for result in results],
        in_specs=[hbm] * 6,
        out_specs=[vmem] * 4,
        scratch_shapes=[
            pltpu.VMEM((3, ROWS, 512), BF16),
            pltpu.VMEM((1, 8192), jnp.int32),
            pltpu.VMEM((512, 1024), BF16),
            pltpu.VMEM((ROWS, 1024), BF16),
            pltpu.VMEM((ROWS, 512), BF16),
            pltpu.VMEM((XS, 2, ROWS, 512), BF16),
            pltpu.VMEM((XS, 2) + tile, BF16),
            pltpu.VMEM((XS,) + tile, BF16),
            pltpu.VMEM((XS,) + tile, BF16),
            pltpu.VMEM((2,) + tile, BF16),
            pltpu.VMEM(tile, BF16),
            pltpu.VMEM(tile, BF16),
            pltpu.VMEM((XS, 2) + tile, BF16),
            pltpu.VMEM((XS,) + tile, BF16),
            pltpu.VMEM((XS,) + tile, BF16),
            pltpu.VMEM((3, 2) + tile, BF16),
            pltpu.VMEM((XS,) + tile, BF16),
            pltpu.VMEM((XS, 2) + tile, BF16),
            pltpu.VMEM((3, 2) + tile, BF16),
            pltpu.VMEM((XS,) + tile, BF16),
            pltpu.VMEM((XS, 2) + tile, BF16),
            pltpu.VMEM((3, 2) + tile, BF16),
            pltpu.VMEM((XS, ROWS, 4 * ROWS), F32),
            pltpu.VMEM((7,) + tile, F32),
            pltpu.VMEM((7,) + tile, F32),
            pltpu.VMEM((2, XS) + tile, BF16),
            pltpu.VMEM((8, 32, 128), BF16),
            pltpu.VMEM((7, 32, 128), BF16),
            pltpu.VMEM((8, 32, 128), BF16),
            pltpu.VMEM((7, 32, 128), BF16),
            pltpu.VMEM((32, 128), F32),
            pltpu.VMEM((32, 128), F32),
            pltpu.VMEM((8, 8, 128), F32),
            dma((6,)),
            dma((4,)), dma((4,)),
            dma((4,)), dma((4,)),
            dma((4,)), dma((4,)),
            dma((3,)), dma((3,)),
            dma, dma,
            dma((2, 3)), dma((2, 3)),
            dma, dma,
            dma((4,)), dma((4,)),
            dma((4,)), dma((4,)),
            dma((3,)), dma((3,)),
            dma((7,)), dma((7,)),
            dma((7,)), dma((7,)),
            dma((8,)), dma((8,)),
            pltpu.SemaphoreType.REGULAR,
        ],
        compiler_params=pltpu.CompilerParams(
            collective_id=0, has_side_effects=True, vmem_limit_bytes=32 * 1024 * 1024
        ),
        cost_estimate=pl.CostEstimate(
            flops=600_000_000, bytes_accessed=4_000_000, transcendentals=262_144
        ),
    )(*operands)
    query_grad, key_grad, value_grad, weight_grad = pl.pallas_call(
        finish,
        out_shape=results,
        in_specs=[vmem] * 4,
        out_specs=[hbm] * 4,
        scratch_shapes=[dma((4,))],
        compiler_params=pltpu.CompilerParams(vmem_limit_bytes=4 * 1024 * 1024),
        cost_estimate=pl.CostEstimate(flops=0, bytes_accessed=1_600_000, transcendentals=0),
    )(*outs)
    return (query_grad[None], key_grad[None], value_grad[None], weight_grad)


def solution(mesh):
    in_specs = (
        P("dp", "cp", None),
        P("dp", "cp", None),
        P("dp", "cp", None),
        P("dp", None),
        P(),
        P("dp", "cp", None),
    )
    out_specs = (P("dp", "cp", None), P("dp", "cp", None), P("dp", "cp", None), P("cp", "dp"))
    return jax.shard_map(body, mesh=mesh, in_specs=in_specs, out_specs=out_specs, check_vma=False)
```
